32 devices in a mesh: dp: 16 (over z, x, core), tensor: 2 (over y).
Axes of the slice: x: 2, y: 2, z: 4, core: 2. Of those that a mesh axis runs over, the one named last changes fastest.
Arguments:
- layer_in: bfloat16 [16, 2, 1024, 768], P(None, 'tensor', 'dp'), may hold values from -6 to 6
- out_grad: bfloat16 [16, 2, 1024, 768], P(None, 'tensor', 'dp'), may hold values from -6 to 6
- seq_lengths: int32 [16], replicated, may hold values from 1 to 2048, 20480 in all
- slot_perm: int32 [16], replicated, may hold values from 0 to 15, each once
- norm_gain: float32 [768], replicated, may hold values from 0.1 to 1.9
- w_gate: bfloat16 [768, 1536], P('dp', 'tensor'), may hold values from -0.21875 to 0.21875
- w_inner: bfloat16 [768, 1536], P('dp', 'tensor'), may hold values from -0.21875 to 0.21875
- w_bc: bfloat16 [768, 128], P('dp'), may hold values from -0.21875 to 0.21875
- w_dt: bfloat16 [768, 48], P('dp', 'tensor'), may hold values from -0.21875 to 0.21875
- conv_x: float32 [4, 1536], P(None, 'tensor'), may hold values from -3 to 3
- conv_bc: float32 [4, 128], replicated, may hold values from -2 to 2
- dt_bias: float32 [48], P('tensor'), may hold values from -4 to -2
- a_log: float32 [24], P('tensor'), may hold values from -4.5 to 0.5
- dskip: float32 [24], P('tensor'), may hold values from 1 to 3
- inner_gain: float32 [1536], P('tensor'), may hold values from 0.1 to 1.9
- w_out: bfloat16 [1536, 768], P('tensor', 'dp'), may hold values from -0.15625 to 0.15625
Outputs:
- output: bfloat16 [16, 2, 1024, 768], P(None, 'tensor', 'dp')
- input_grad: bfloat16 [16, 2, 1024, 768], P(None, 'tensor', 'dp')
- grad_norm_gain: float32 [768], replicated
- grad_w_gate: float32 [768, 1536], P('dp', 'tensor')
- grad_w_inner: float32 [768, 1536], P('dp', 'tensor')
- grad_w_bc: float32 [768, 128], P('dp')
- grad_w_dt: float32 [768, 48], P('dp', 'tensor')
- grad_conv_x: float32 [4, 1536], P(None, 'tensor')
- grad_conv_bc: float32 [4, 128], replicated
- grad_dt_bias: float32 [48], P('tensor')
- grad_a_log: float32 [24], P('tensor')
- grad_dskip: float32 [24], P('tensor')
- grad_inner_gain: float32 [1536], P('tensor')
- grad_w_out: float32 [1536, 768], P('tensor', 'dp')
The draws below stay inside these ranges and needn't reach their ends.
Inputs may be any that keep to these rules, and one draw needn't show every extreme that they name: Sequence s is computed in slot slot_perm[s]; slot i belongs to index i of dp; out_grad, output and input_grad are indexed by slot. `seq_lengths`: some sequence has exactly 2048 valid positions.
All inputs are finite; a program needn't handle non-finite values.
Results may differ from the reference program's by a relative error of at most 0.011.
Values may be sent and summed in bfloat16 or wider, within the bound.
No kernel may reach another device: no remote copies, remote signals or barrier semaphores. Data moves between devices by JAX's collectives and lax.ppermute only.
A program may use at most 320 MiB of HBM per device.

```python
import math
import jax
import jax.numpy as jnp
import numpy as np
from jax import lax

D = 768
HEADS = 24
STATE = 64
CONV = 4
BLOCK = 128
LEN = 2048
INNER = 1536
SEQS = 16
HALF = 1024
N_TENSOR = 2


def shard_levels(stream_key, dims, pieces, least, largest):
    def one(axis_at, parts):
        steps = jax.random.uniform(jax.random.fold_in(jax.random.fold_in(stream_key, 6), axis_at), (parts,), jnp.float32, least / len(pieces), largest / len(pieces))
        return jnp.repeat(jnp.exp(steps), dims[axis_at] // parts).reshape((-1,) + (1,) * (len(dims) - axis_at - 1))

    level = one(*pieces[0])
    for cut in pieces[1:]:
        level = level * one(*cut)
    return level


def split_up(count, total, limit, lean):
    loads = [(1 << 20) // math.isqrt(standing ** lean) + 1 for standing in range(2, count + 1)]
    surplus, counts = total - limit - (count - 1), [1] * (count - 1)
    while surplus > 0:
        movable = [i for i in range(count - 1) if counts[i] < limit]
        mass, budget = sum([loads[i] for i in movable]), surplus
        for i in movable:
            addition = min(limit - counts[i], max(1, budget * loads[i] // mass), surplus)
            counts[i] = counts[i] + addition
            surplus = surplus - addition
    return np.array([limit] + counts)


def ragged(rng, amount, total, limit, slope):
    if amount == 2:
        one = jax.random.randint(rng, (), max(1, total - limit), min(limit, total - 1) + 1)
        return jnp.stack([one, total - one])
    lengths = jnp.asarray(split_up(amount, total, limit, slope), jnp.int32)
    twos = (amount - 1) // 2
    donor, receiver = lengths[1:1 + 2 * twos:2], lengths[2:2 + 2 * twos:2]
    margin = jnp.minimum(donor - 1, limit - receiver)
    moved = jax.random.randint(jax.random.fold_in(rng, 1), (twos,), 0, 1 << 20) % (margin + 1)
    lengths = lengths.at[1:1 + 2 * twos:2].set(donor - moved).at[2:2 + 2 * twos:2].set(receiver + moved)
    return lengths[jax.random.permutation(jax.random.fold_in(rng, 2), amount)]


def scatter_about(own_key, shape, scale, reach, split=(), held_as=jnp.bfloat16):
    gain = shard_levels(own_key, shape, split, -0.22, 0.18) if split else 1.0
    values = jax.random.normal(own_key, shape, jnp.float32) * scale * gain
    return jnp.minimum(jnp.maximum(values, -reach), reach).astype(held_as)


def setup_inputs(seed: int = 0) -> dict:
    key_list = jax.random.split(jax.random.key(seed), 17)
    layer_in = scatter_about(key_list[0], (SEQS, N_TENSOR, HALF, D), 1.0, 6.0, ((1, 2), (2, 16)))
    out_grad = scatter_about(key_list[1], (SEQS, N_TENSOR, HALF, D), 1.0, 6.0, ((1, 2), (2, 16)))
    seq_lengths = ragged(key_list[2], SEQS, SEQS * LEN * 5 // 8, LEN, 2).astype(jnp.int32)
    slot_perm = jax.random.permutation(key_list[3], SEQS).astype(jnp.int32)
    norm_gain = jnp.clip(1.0 + 0.18 * jax.random.normal(key_list[4], (D,), jnp.float32), 0.1, 1.9)
    w_gate = scatter_about(key_list[5], (D, INNER), D ** -0.5, 0.21875, ((0, 16), (1, 2)))
    w_inner = scatter_about(key_list[6], (D, INNER), D ** -0.5, 0.21875, ((0, 16), (1, 2)))
    w_bc = scatter_about(key_list[7], (D, 2 * STATE), D ** -0.5, 0.21875, ((0, 16),))
    w_dt = scatter_about(key_list[8], (D, 2 * HEADS), D ** -0.5, 0.21875, ((0, 16), (1, 2)))
    conv_x = scatter_about(key_list[9], (CONV, INNER), 0.5, 3.0, ((1, 2),), jnp.float32)
    conv_bc = scatter_about(key_list[10], (CONV, 2 * STATE), 0.3, 2.0, (), jnp.float32)
    dt_bias = jnp.clip(-4.0 + 2.0 * jax.random.uniform(key_list[11], (2 * HEADS,), jnp.float32) ** shard_levels(key_list[11], (2 * HEADS,), ((0, 2),), -0.2, 0.2), -4.0, -2.0)
    a_log = jnp.clip(-4.5 + 5.0 * jax.random.uniform(key_list[12], (HEADS,), jnp.float32) ** shard_levels(key_list[12], (HEADS,), ((0, 2),), -0.2, 0.2), -4.5, 0.5)
    dskip = jnp.clip(1.0 + 2.0 * jax.random.uniform(key_list[13], (HEADS,), jnp.float32) ** shard_levels(key_list[13], (HEADS,), ((0, 2),), -0.2, 0.2), 1.0, 3.0)
    inner_gain = jnp.clip(1.0 + 0.18 * jax.random.normal(key_list[14], (INNER,), jnp.float32), 0.1, 1.9)
    w_out = scatter_about(key_list[15], (INNER, D), INNER ** -0.5, 0.15625, ((0, 2), (1, 16)))
    return {"layer_in": layer_in, "out_grad": out_grad, "seq_lengths": seq_lengths, "slot_perm": slot_perm, "norm_gain": norm_gain, "w_gate": w_gate, "w_inner": w_inner, "w_bc": w_bc, "w_dt": w_dt, "conv_x": conv_x, "conv_bc": conv_bc, "dt_bias": dt_bias, "a_log": a_log, "dskip": dskip, "inner_gain": inner_gain, "w_out": w_out}


exact_prec = lax.Precision.HIGHEST

@jax.custom_vjp
def low(v):
    return lax.optimization_barrier(v.astype(jnp.bfloat16)).astype(jnp.float32)

@jax.custom_vjp
def low_back(v):
    return v

def low_keep(v):
    return (low(v), None)

def low_pass(kept, grad):
    return (grad,)

def back_keep(v):
    return (v, None)

def back_low(kept, grad):
    return (low(grad),)
low.defvjp(low_keep, low_pass)
low_back.defvjp(back_keep, back_low)

def causal_conv(values, kernel):
    taps_count = kernel.shape[0]
    length = values.shape[0]
    padded = jnp.pad(values, ((taps_count - 1, 0), (0, 0)))
    summed = jnp.zeros(values.shape, jnp.float32)
    for offset in range(taps_count):
        summed = summed + kernel[offset] * padded[offset:offset + length]
    return summed

def strict_scan(values, state_in, state_out, log_decay):
    length, head_count, head_width = values.shape
    blocks = length // BLOCK
    blocked = values.reshape(blocks, BLOCK, head_count, head_width)
    in_maps = state_in.reshape(blocks, BLOCK, -1)
    out_maps = state_out.reshape(blocks, BLOCK, -1)
    partial_sums = jnp.cumsum(log_decay.reshape(blocks, BLOCK, head_count), axis=1)
    scores = jnp.einsum('kin,kjn->kij', out_maps, in_maps, precision=exact_prec)
    row_ids = lax.broadcasted_iota(jnp.int32, (BLOCK, BLOCK), 0)
    col_ids = lax.broadcasted_iota(jnp.int32, (BLOCK, BLOCK), 1)
    lower = (row_ids > col_ids)[None, :, :, None]
    spread = partial_sums[:, :, None, :] - partial_sums[:, None, :, :]
    decay = jnp.where(lower, jnp.exp(jnp.where(lower, spread, 0.0)), 0.0)
    weights_in = scores[..., None] * decay
    inside = jnp.einsum('kijh,kjhp->kihp', weights_in, blocked, precision=exact_prec)
    to_end = jnp.exp(partial_sums[:, -1:, :] - partial_sums)
    block_states = jnp.einsum('kjn,kjhp->khnp', in_maps, blocked * to_end[..., None], precision=exact_prec)
    block_decay = jnp.exp(partial_sums[:, -1, :])

    def carry_step(carried, item):
        decay_now, state_now = item
        return (carried * decay_now[:, None, None] + state_now, carried)
    start_state = jnp.zeros(block_states.shape[1:], jnp.float32)
    _, entering = lax.scan(carry_step, start_state, (block_decay, block_states))
    outside = jnp.einsum('kin,khnp->kihp', out_maps, entering, precision=exact_prec)
    outside = outside * jnp.exp(partial_sums)[..., None]
    return (inside + outside).reshape(length, head_count, head_width)

def mixer(inner_in, bc_raw, step_raw, gate, conv_x, conv_bc, dt_bias, a_log, dskip, inner_gain, mask):
    length = inner_in.shape[0]
    head_count = a_log.shape[0]
    head_width = inner_in.shape[1] // head_count
    conv_out = jax.nn.silu(causal_conv(inner_in, conv_x))
    bc_conv = jax.nn.silu(causal_conv(bc_raw, conv_bc))
    state_width = bc_conv.shape[1] // 2
    state_in = bc_conv[:, :state_width]
    state_out = bc_conv[:, state_width:]
    step_size = jax.nn.softplus(step_raw + dt_bias).reshape(length, head_count, 2)
    log_decay = -step_size * jnp.exp(a_log)[None, :, None]
    heads_x = conv_out.reshape(length, head_count, head_width)
    forward_v = (mask[:, None] * step_size[:, :, 0])[:, :, None] * heads_x
    backward_v = (mask[:, None] * step_size[:, :, 1])[:, :, None] * heads_x
    forward_out = strict_scan(forward_v, state_in, state_out, log_decay[:, :, 0])
    backward_out = jnp.flip(strict_scan(jnp.flip(backward_v, 0), jnp.flip(state_in, 0), jnp.flip(state_out, 0), jnp.flip(log_decay[:, :, 1], 0)), 0)
    mixture = forward_out + backward_out + dskip[None, :, None] * heads_x
    gated_out = mixture * jax.nn.silu(gate.reshape(length, head_count, head_width))
    scaled = gated_out * lax.rsqrt(lax.optimization_barrier(jnp.mean(gated_out * gated_out, axis=-1, keepdims=True)) + 1e-05)
    return (scaled * inner_gain.reshape(head_count, head_width)).reshape(length, head_count * head_width)

def layer(params, rows, mask):
    norm_gain, w_gate, w_inner, w_bc, w_dt, conv_x, conv_bc, dt_bias, a_log, dskip, inner_gain, w_out = params
    inv_rms = lax.rsqrt(lax.optimization_barrier(jnp.mean(rows * rows, axis=-1, keepdims=True)) + 1e-05)
    normed = low(rows * inv_rms * norm_gain)
    gate = low_back(jnp.dot(normed, w_gate, precision=exact_prec))
    inner_in = low_back(jnp.dot(normed, w_inner, precision=exact_prec))
    bc_raw = low_back(jnp.dot(normed, w_bc, precision=exact_prec))
    step_raw = low_back(jnp.dot(normed, w_dt, precision=exact_prec))
    result = low(low_back(mixer(inner_in, bc_raw, step_raw, gate, conv_x, conv_bc, dt_bias, a_log, dskip, inner_gain, mask)))
    return rows + mask[:, None] * jnp.dot(result, w_out, precision=exact_prec)

def reference(layer_in, out_grad, seq_lengths, slot_perm, norm_gain, w_gate, w_inner, w_bc, w_dt, conv_x, conv_bc, dt_bias, a_log, dskip, inner_gain, w_out):
    params = tuple((item.astype(jnp.float32) for item in (norm_gain, w_gate, w_inner, w_bc, w_dt, conv_x, conv_bc, dt_bias, a_log, dskip, inner_gain, w_out)))
    rows_all = layer_in.astype(jnp.float32).reshape(SEQS, LEN, D)
    grads_slot = out_grad.astype(jnp.float32).reshape(SEQS, LEN, D)
    grads_all = jnp.take(grads_slot, slot_perm.astype(jnp.int32), axis=0)
    positions = jnp.arange(LEN, dtype=jnp.int32)

    def one_sequence(totals, item):
        rows, cotangent, length = item
        mask = (positions < length).astype(jnp.float32)
        output, pull = jax.vjp(lambda weights, inputs: layer(weights, inputs, mask), params, rows)
        grad_params, grad_rows = pull(cotangent)
        totals = jax.tree.map(lambda first, second: first + second, totals, grad_params)
        return (totals, (output.astype(jnp.bfloat16), grad_rows.astype(jnp.bfloat16)))
    zeros = jax.tree.map(jnp.zeros_like, params)
    totals, (outputs, in_grads) = lax.scan(one_sequence, zeros, (rows_all, grads_all, seq_lengths))
    slots = slot_perm.astype(jnp.int32)
    outputs = jnp.zeros_like(outputs).at[slots].set(outputs)
    in_grads = jnp.zeros_like(in_grads).at[slots].set(in_grads)
    shape = (SEQS, N_TENSOR, HALF, D)
    return (outputs.reshape(shape), in_grads.reshape(shape), totals[0], totals[1], totals[2], totals[3], totals[4], totals[5], totals[6], totals[7], totals[8], totals[9], totals[10], totals[11])
```

```python
import functools
import jax
import jax.numpy as jnp
from jax import lax
from jax.experimental import pallas as pl
from jax.experimental.pallas import tpu as pltpu
from jax.sharding import Mesh
from jax.sharding import PartitionSpec as P

F32 = jnp.float32
BF = jnp.bfloat16
CH = 128
BLK = 256
ZR = 32
HIGH = lax.Precision.HIGHEST
VMEM_LIMIT = 60 * 1024 * 1024


def nn(a, b):
    return lax.dot_general(a, b, (((1,), (0,)), ((), ())), preferred_element_type=F32)


def nt(a, b):
    return lax.dot_general(a, b, (((1,), (1,)), ((), ())), preferred_element_type=F32)


def tn(a, b):
    return lax.dot_general(a, b, (((0,), (0,)), ((), ())), preferred_element_type=F32)


def running(rows, tri):
    return lax.dot_general(rows, tri, (((1,), (0,)), ((), ())), precision=HIGH, preferred_element_type=F32)


def softplus(z):
    return jnp.maximum(z, 0.0) + jnp.log1p(jnp.exp(-jnp.abs(z)))


def sigmoid(v):
    return 1.0 / (1.0 + jnp.exp(-v))


def tri(cond):
    r = lax.broadcasted_iota(jnp.int32, (CH, CH), 0)
    c = lax.broadcasted_iota(jnp.int32, (CH, CH), 1)
    return jnp.where(cond(r, c), 1.0, 0.0).astype(F32)


def interleave(core, a_ref, b_ref):
    parts = []
    for i in range(a_ref.shape[0]):
        a, b = a_ref[i].astype(F32), b_ref[i].astype(F32)
        parts += [jnp.where(core == 0, a, b), jnp.where(core == 0, b, a)]
    return jnp.concatenate(parts, 0)


def split_rows(core, v, own_ref, oth_ref):
    width = own_ref.shape[1]
    for i in range(own_ref.shape[0]):
        e = v[2 * i * width : (2 * i + 1) * width]
        o = v[(2 * i + 1) * width : (2 * i + 2) * width]
        own_ref[i] = jnp.where(core == 0, e, o).astype(own_ref.dtype)
        oth_ref[i] = jnp.where(core == 0, o, e).astype(oth_ref.dtype)


def decays(z, alog, mask):
    dt = softplus(z)
    a = -jnp.exp(alog) * dt
    cs = running(a, tri(lambda r, c: r <= c))
    return dt * mask, a, cs


def enter(meta, xa, xb, w, gain, taps, bias, alog, nrm, gate, ain, u, zt, sf, wt, halo, state, vfe):
    j = pl.program_id(0)
    core, length = meta[0], meta[1]
    dm = w.shape[0]
    inner = gate.shape[0]
    heads = inner // 64
    cat = inner + 2 * 64
    top = inner

    @pl.when(j == 0)
    def _():
        wt[0 : 2 * inner + 128, :] = w[:, inner : 3 * inner + 128].T
        wt[2 * inner + 128 : 2 * inner + 128 + ZR, :] = w[:, 3 * inner + 128 : 3 * inner + 256].T[0:ZR]
        halo[...] = jnp.zeros_like(halo)
        state[...] = jnp.zeros_like(state)

    x = interleave(core, xa, xb)
    r = lax.rsqrt(jnp.mean(x * x, axis=-1, keepdims=True) + 1e-05)
    normed = (x * r * gain[...]).astype(BF)
    nrm[...] = normed
    gate[...] = nt(wt[0:top, :], normed)
    for g in range(0, cat, 128):
        cur = nt(wt[top + g : top + g + 128, :], normed)
        full = jnp.concatenate([halo[g : g + 128, :], cur], 1)
        halo[g : g + 128, :] = cur[:, BLK - 128 :]
        ain[g : g + 128, :] = cur.astype(ain.dtype)
        t = taps[g : g + 128, :]
        acc = t[:, 3:4] * cur
        for k in (1, 2, 3):
            acc = acc + t[:, 3 - k : 4 - k] * pltpu.roll(full, k, 1)[:, 128:]
        u[g : g + 128, :] = acc
    z = nt(wt[top + cat : top + cat + ZR, :], normed) + bias[...]
    zt[...] = z
    for q in range(BLK // CH):
        lanes = slice(q * CH, (q + 1) * CH)
        pos = j * BLK + q * CH + lax.broadcasted_iota(jnp.int32, (1, CH), 1)
        mask = jnp.where(pos < length, 1.0, 0.0)
        mdt, a, cs = decays(z[:, lanes], alog[...], mask)
        tot = cs[:, CH - 1 : CH]
        wrow = mdt * jnp.exp(tot - cs)
        etot = jnp.exp(tot)
        bu = u[inner : inner + 64, lanes]
        bt = (bu * sigmoid(bu)).astype(BF)
        for h in range(heads):
            hs = slice(64 * h, 64 * h + 64)
            uh = u[hs, lanes]
            vfe[hs, :] = (uh * sigmoid(uh) * wrow[h : h + 1, :]).astype(BF)
        add = nt(vfe[...], bt)
        for h in range(heads):
            hs = slice(64 * h, 64 * h + 64)
            sf[q, hs, :] = state[hs, :].astype(sf.dtype)
            state[hs, :] = state[hs, :] * etot[h : h + 1, :] + add[hs, :]


def mix(meta, dskip, dya, dyb, wot, gate, u, zt, sf, gain, alog, own, oth, dgate, dxp, ddt, dap, dbc, zb, sbin, gwo, dgain, dsk, wo, gacc, gy, ynt, yin, dv, dye, vfe, vbe, sb, dsf, rows):
    i = pl.program_id(0)
    last = pl.num_programs(0) - 1
    j = last - i
    core, length = meta[0], meta[1]
    inner = gate.shape[0]
    heads = inner // 64

    @pl.when(i == 0)
    def _():
        wo[...] = wot[...].T
        gacc[...] = jnp.zeros_like(gacc)
        sb[...] = jnp.zeros_like(sb)
        dsf[...] = jnp.zeros_like(dsf)
        dgain[...] = jnp.zeros_like(dgain)
        dsk[...] = jnp.zeros_like(dsk)

    cot = interleave(core, dya, dyb)
    rowpos = j * BLK + lax.broadcasted_iota(jnp.int32, (BLK, 1), 0)
    cot = jnp.where(rowpos < length, cot, 0.0).astype(BF)
    gy[...] = nt(wo[...], cot).astype(BF).astype(F32)
    low = lax.broadcasted_iota(jnp.int32, (CH, CH), 0) > lax.broadcasted_iota(jnp.int32, (CH, CH), 1)
    up = lax.broadcasted_iota(jnp.int32, (CH, CH), 0) < lax.broadcasted_iota(jnp.int32, (CH, CH), 1)
    for q in reversed(range(BLK // CH)):
        lanes = slice(q * CH, (q + 1) * CH)
        pos = j * BLK + q * CH + lax.broadcasted_iota(jnp.int32, (1, CH), 1)
        mask = jnp.where(pos < length, 1.0, 0.0)
        mdt, a, cs = decays(zt[:, lanes], alog[...], mask)
        csf = cs[0:16]
        ecb = cs[16:32] - a[16:32]
        totf = cs[0:16, CH - 1 : CH]
        totb = cs[16:32, CH - 1 : CH]
        ccf = csf.T
        ccb = ecb.T
        ef = jnp.exp(csf)
        wf = jnp.exp(totf - csf)
        eb = jnp.exp(totb - ecb)
        wb = jnp.exp(ecb)
        etf = jnp.exp(totf)
        etb = jnp.exp(totb)
        bu = u[inner : inner + 64, lanes]
        cu = u[inner + 64 : inner + 128, lanes]
        bt = (bu * sigmoid(bu)).astype(BF)
        ct = (cu * sigmoid(cu)).astype(BF)
        gmat = tn(ct, bt)
        glow = jnp.where(low, gmat, 0.0)
        gup = jnp.where(up, gmat, 0.0)
        sbb = sb[...].astype(BF)
        sbin[q] = sbb
        dsb = dsf[...].astype(BF)
        yin[0:inner, :] = nn(sf[q], ct)
        yin[inner : 2 * inner, :] = nn(sbb, ct)
        dv[...] = nn(dsb, bt)
        dg_sum = jnp.zeros((CH, CH), F32)
        for h in range(heads):
            hs = slice(64 * h, 64 * h + 64)
            h1 = slice(h, h + 1)
            uh = u[hs, lanes]
            x = uh * sigmoid(uh)
            mf = mdt[h : h + 1, :]
            mb = mdt[16 + h : 17 + h, :]
            vf = x * mf
            vb = x * mb
            vf16 = vf.astype(BF)
            vb16 = vb.astype(BF)
            pm = jnp.exp(jnp.where(low, ccf[:, h1] - csf[h1, :], ecb[h1, :] - ccb[:, h1]))
            ml = (pm * glow).astype(BF)
            mu = (pm * gup).astype(BF)
            ybi = yin[inner + 64 * h : inner + 64 * h + 64, :] * eb[h1, :]
            yf = nt(vf16, ml) + yin[hs, :] * ef[h1, :]
            yb = nt(vb16, mu) + ybi
            yt = yf + yb + dskip[h] * x
            gt = gate[hs, lanes]
            sg = sigmoid(gt)
            sl = gt * sg
            g = yt * sl
            ri = lax.rsqrt(jnp.mean(g * g, axis=0, keepdims=True) + 1e-05)
            gh = g * ri
            gn = gain[hs, :]
            ynt[hs, lanes] = (gh * gn).astype(BF)
            gyh = gy[hs, lanes]
            dgain[hs, :] += gyh * gh
            ds = gyh * gn
            dg = ri * (ds - gh * jnp.mean(ds * gh, axis=0, keepdims=True))
            dgate[hs, lanes] = (dg * yt * (sg * (1.0 + gt * (1.0 - sg)))).astype(BF)
            dy = dg * sl
            dyb16 = dy.astype(BF)
            dvi = dv[hs, :] * wf[h1, :]
            dvf = nn(dyb16, ml) + dvi
            dvb = nn(dyb16, mu)
            dyr = dyb16.astype(F32)
            vfr = vf16.astype(F32)
            qm = tn(dyb16, x.astype(BF))
            dg_sum = dg_sum + qm * pm * jnp.where(low, mf, mb)
            sxf = jnp.sum(x * dvf, axis=0, keepdims=True)
            sxb = jnp.sum(x * dvb, axis=0, keepdims=True)
            rows[0, h1, :] = sxf
            rows[1, h1, :] = sxb
            rows[2, h1, :] = jnp.sum(dyr * yf - vfr * dvf, axis=0, keepdims=True)
            rows[3, h1, :] = jnp.sum(vb16.astype(F32) * dvb - dyr * yb, axis=0, keepdims=True)
            prod = jnp.sum(dsf[hs, :] * sf[q, hs, :].astype(F32), axis=0, keepdims=True)
            prod = jnp.sum(prod, axis=1, keepdims=True) * etf[h1, :]
            rows[4, h1, :] = jnp.sum(vfr * dvi, axis=0, keepdims=True) + prod * (1.0 / CH)
            rows[5, h1, :] = jnp.sum(dyr * ybi, axis=0, keepdims=True)
            dsk[h1, :] += jnp.sum(dy * x, axis=0, keepdims=True)
            dxp[hs, lanes] = dskip[h] * dy + mf * dvf + mb * dvb
            dye[hs, :] = (dy * ef[h1, :]).astype(BF)
            dye[inner + 64 * h : inner + 64 * h + 64, :] = (dy * eb[h1, :]).astype(BF)
            vfe[hs, :] = (vf * wf[h1, :]).astype(BF)
            vbe[hs, :] = (vb * wb[h1, :]).astype(BF)
        dgb = jnp.where(low | up, dg_sum, 0.0).astype(BF)
        dbc[64:128, lanes] = nt(bt, dgb) + tn(sf[q], dye[0:inner, :]) + tn(sbb, dye[inner : 2 * inner, :])
        dbc[0:64, lanes] = nn(ct, dgb) + tn(dsb, vfe[...])
        grow = nt(dye[...], ct)
        srow = nt(vbe[...], bt)
        zb[q] = grow[inner : 2 * inner, :].astype(zb.dtype)
        for h in range(heads):
            hs = slice(64 * h, 64 * h + 64)
            dsf[hs, :] = dsf[hs, :] * etf[h : h + 1, :] + grow[hs, :]
            sb[hs, :] = sb[hs, :] * etb[h : h + 1, :] + srow[hs, :]
        ddt[0:16, lanes] = rows[0] * mask
        ddt[16:32, lanes] = rows[1] * mask
        dap[0:16, lanes] = running(rows[2], tri(lambda r, c: r >= c)) + jnp.sum(rows[4], axis=1, keepdims=True)
        dap[16:32, lanes] = running(rows[3], tri(lambda r, c: r > c)) + jnp.sum(rows[5], axis=1, keepdims=True)
    o = tn(ynt[...], wo[...])
    split_rows(core, o, own, oth)
    gacc[...] += nn(ynt[...], cot)

    @pl.when(i == last)
    def _():
        gwo[...] = gacc[...].T.astype(gwo.dtype)


def carry(meta, u, zt, alog, dxp, ddt, dap, dbc, zb, sbin, du, dz, dbias, dal, dsb, dvs, vbe, row):
    j = pl.program_id(0)
    length = meta[1]
    inner = dxp.shape[0]
    heads = inner // 64

    @pl.when(j == 0)
    def _():
        dsb[...] = jnp.zeros_like(dsb)
        dbias[...] = jnp.zeros_like(dbias)
        dal[...] = jnp.zeros_like(dal)
        row[...] = jnp.zeros_like(row)

    for q in range(BLK // CH):
        lanes = slice(q * CH, (q + 1) * CH)
        pos = j * BLK + q * CH + lax.broadcasted_iota(jnp.int32, (1, CH), 1)
        mask = jnp.where(pos < length, 1.0, 0.0)
        z = zt[:, lanes]
        mdt, a, cs = decays(z, alog[...], mask)
        ecb = cs[16:32] - a[16:32]
        etb = jnp.exp(cs[16:32, CH - 1 : CH])
        wb = jnp.exp(ecb)
        mw = mdt[16:32] * wb
        bu = u[inner : inner + 64, lanes]
        cu = u[inner + 64 : inner + 128, lanes]
        sgb = sigmoid(bu)
        sgc = sigmoid(cu)
        bt = (bu * sgb).astype(BF)
        dsb16 = dsb[...].astype(BF)
        dvs[...] = nn(dsb16, bt)
        for h in range(heads):
            hs = slice(64 * h, 64 * h + 64)
            h1 = slice(h, h + 1)
            uh = u[hs, lanes]
            sg = sigmoid(uh)
            x = uh * sg
            raw = dvs[hs, :]
            row[0, h1, :] = jnp.sum(x * raw, axis=0, keepdims=True) * wb[h1, :]
            prod = jnp.sum(dsb[hs, :] * sbin[q, hs, :].astype(F32), axis=0, keepdims=True)
            row[1, h1, :] = jnp.broadcast_to(jnp.sum(prod, axis=1, keepdims=True) * etb[h1, :], (1, CH))
            dx = dxp[hs, lanes] + raw * mw[h1, :]
            du[hs, lanes] = dx * (sg * (1.0 + uh * (1.0 - sg)))
            vbe[hs, :] = (x * mw[h1, :]).astype(BF)
        db = dbc[0:64, lanes] + tn(dsb16, vbe[...])
        du[inner : inner + 64, lanes] = db * (sgb * (1.0 + bu * (1.0 - sgb)))
        du[inner + 64 : inner + 128, lanes] = dbc[64:128, lanes] * (sgc * (1.0 + cu * (1.0 - sgc)))
        for h in range(heads):
            hs = slice(64 * h, 64 * h + 64)
            dsb[hs, :] = dsb[hs, :] * etb[h : h + 1, :] + zb[q, hs, :].astype(F32)
        dab = dap[16:32, lanes] + running(mdt[16:32] * row[0], tri(lambda r, c: r > c)) + row[1]
        da = jnp.concatenate([dap[0:16, lanes], dab], 0)
        dd = jnp.concatenate([ddt[0:16, lanes], ddt[16:32, lanes] + row[0] * mask], 0)
        dal[...] += da * a
        dzz = (dd - jnp.exp(alog[...]) * da) * sigmoid(z)
        dbias[...] += dzz
        dz[:, lanes] = dzz.astype(dz.dtype)


def leave(meta, du, nxt, ain, dgate, dz, nrm, wt, taps, own, oth, gw, dtaps, acc, cat):
    j = pl.program_id(0)
    last = pl.num_programs(0) - 1
    core = meta[0]
    inner = dgate.shape[0]
    conv = inner + 128

    @pl.when(j == 0)
    def _():
        acc[...] = jnp.zeros_like(acc)
        dtaps[...] = jnp.zeros_like(dtaps)

    cat[0:inner, :] = dgate[...]
    for g in range(0, conv, 128):
        cur = du[g : g + 128, :]
        after = jnp.where(j == last, 0.0, nxt[g : g + 128, :])
        full = jnp.concatenate([cur, after], 1)
        a = ain[g : g + 128, :].astype(F32)
        t = taps[g : g + 128, :]
        total = t[:, 3:4] * cur
        p = a * cur
        dtaps[3, g : g + 128, :] += p[:, 0:128] + p[:, 128:256]
        for k in (1, 2, 3):
            moved = pltpu.roll(full, BLK + 128 - k, 1)[:, 0:BLK]
            total = total + t[:, 3 - k : 4 - k] * moved
            p = a * moved
            dtaps[3 - k, g : g + 128, :] += p[:, 0:128] + p[:, 128:256]
        cat[inner + g : inner + g + 128, :] = total.astype(BF)
    cat[inner + conv : inner + conv + ZR, :] = dz[...]
    gn = tn(cat[...], wt[...])
    split_rows(core, gn, own, oth)
    acc[...] += nn(cat[...], nrm[...])

    @pl.when(j == last)
    def _():
        gw[...] = acc[...].T.astype(gw.dtype)


def _params():
    return pltpu.CompilerParams(dimension_semantics=("arbitrary",), vmem_limit_bytes=VMEM_LIMIT)


def full(shape):
    return pl.BlockSpec(shape, lambda j, *_: (0,) * len(shape))


def sds(shape, dt):
    return jax.ShapeDtypeStruct(shape, dt)


def run_enter(meta, xa, xb, wpack, gain, taps, bias, alog):
    nblk, width, dm = xa.shape
    length = 2 * nblk * width
    inner = taps.shape[0] - 128
    nk = BLK // (2 * width)
    nb = length // BLK
    rowsb = pl.BlockSpec((nk, width, dm), lambda j, *_: (j, 0, 0))
    colb = lambda n: pl.BlockSpec((n, BLK), lambda j, *_: (0, j))
    wrows = 2 * inner + 128 + ZR
    return pl.pallas_call(
        enter,
        grid_spec=pltpu.PrefetchScalarGridSpec(
            num_scalar_prefetch=1,
            grid=(nb,),
            in_specs=[rowsb, rowsb, full(wpack.shape), full(gain.shape), full(taps.shape), full(bias.shape), full(alog.shape)],
            out_specs=[
                pl.BlockSpec((BLK, dm), lambda j, *_: (j, 0)),
                colb(inner),
                colb(inner + 128),
                colb(inner + 128),
                colb(ZR),
                pl.BlockSpec((BLK // CH, inner, 64), lambda j, *_: (j, 0, 0)),
                full((wrows, dm)),
            ],
            scratch_shapes=[
                pltpu.VMEM((inner + 128, 128), F32),
                pltpu.VMEM((inner, 64), F32),
                pltpu.VMEM((inner, CH), BF),
            ],
        ),
        out_shape=[
            sds((length, dm), BF),
            sds((inner, length), F32),
            sds((inner + 128, length), BF),
            sds((inner + 128, length), F32),
            sds((ZR, length), F32),
            sds((length // CH, inner, 64), BF),
            sds((wrows, dm), BF),
        ],
        compiler_params=_params(),
        cost_estimate=pl.CostEstimate(flops=2 * length * dm * wrows, bytes_accessed=30_000_000, transcendentals=4 * inner * length),
    )(meta, xa, xb, wpack, gain, taps, bias, alog)


def run_mix(meta, dskip, dya, dyb, wpack, gate, u, zt, sf, gain, alog):
    nblk, width, dm = dya.shape
    length = 2 * nblk * width
    inner = gate.shape[0]
    nk = BLK // (2 * width)
    nb = length // BLK
    rowsb = pl.BlockSpec((nk, width, dm), lambda i, *_: (nb - 1 - i, 0, 0))
    colb = lambda n: pl.BlockSpec((n, BLK), lambda i, *_: (0, nb - 1 - i))
    stb = pl.BlockSpec((BLK // CH, inner, 64), lambda i, *_: (nb - 1 - i, 0, 0))
    return pl.pallas_call(
        mix,
        grid_spec=pltpu.PrefetchScalarGridSpec(
            num_scalar_prefetch=2,
            grid=(nb,),
            in_specs=[rowsb, rowsb, pl.BlockSpec((dm, inner), lambda i, *_: (0, 0)), colb(inner), colb(inner + 128), colb(ZR), stb, full(gain.shape), full(alog.shape)],
            out_specs=[
                rowsb,
                rowsb,
                colb(inner),
                colb(inner),
                colb(ZR),
                colb(ZR),
                colb(128),
                stb,
                stb,
                full((dm, inner)),
                full((inner, CH)),
                full((16, CH)),
            ],
            scratch_shapes=[
                pltpu.VMEM((inner, dm), BF),
                pltpu.VMEM((inner, dm), F32),
                pltpu.VMEM((inner, BLK), F32),
                pltpu.VMEM((inner, BLK), BF),
                pltpu.VMEM((2 * inner, CH), F32),
                pltpu.VMEM((inner, CH), F32),
                pltpu.VMEM((2 * inner, CH), BF),
                pltpu.VMEM((inner, CH), BF),
                pltpu.VMEM((inner, CH), BF),
                pltpu.VMEM((inner, 64), F32),
                pltpu.VMEM((inner, 64), F32),
                pltpu.VMEM((6, 16, CH), F32),
            ],
        ),
        out_shape=[
            sds((nblk, width, dm), F32),
            sds((nblk, width, dm), BF),
            sds((inner, length), BF),
            sds((inner, length), F32),
            sds((ZR, length), F32),
            sds((ZR, length), F32),
            sds((128, length), F32),
            sds((length // CH, inner, 64), BF),
            sds((length // CH, inner, 64), BF),
            sds((dm, inner), BF),
            sds((inner, CH), F32),
            sds((16, CH), F32),
        ],
        compiler_params=_params(),
        cost_estimate=pl.CostEstimate(flops=40 * 10**9, bytes_accessed=50_000_000, transcendentals=10**7),
    )(meta, dskip, dya, dyb, wpack, gate, u, zt, sf, gain, alog)


def run_carry(meta, u, zt, alog, dxp, ddt, dap, dbc, zb, sbin):
    inner, length = dxp.shape
    nb = length // BLK
    colb = lambda n: pl.BlockSpec((n, BLK), lambda j, *_: (0, j))
    stb = pl.BlockSpec((BLK // CH, inner, 64), lambda j, *_: (j, 0, 0))
    return pl.pallas_call(
        carry,
        grid_spec=pltpu.PrefetchScalarGridSpec(
            num_scalar_prefetch=1,
            grid=(nb,),
            in_specs=[colb(inner + 128), colb(ZR), full(alog.shape), colb(inner), colb(ZR), colb(ZR), colb(128), stb, stb],
            out_specs=[colb(inner + 128), colb(ZR), full((ZR, CH)), full((ZR, CH))],
            scratch_shapes=[
                pltpu.VMEM((inner, 64), F32),
                pltpu.VMEM((inner, CH), F32),
                pltpu.VMEM((inner, CH), BF),
                pltpu.VMEM((2, 16, CH), F32),
            ],
        ),
        out_shape=[sds((inner + 128, length), F32), sds((ZR, length), BF), sds((ZR, CH), F32), sds((ZR, CH), F32)],
        compiler_params=_params(),
        cost_estimate=pl.CostEstimate(flops=10**9, bytes_accessed=30_000_000, transcendentals=10**6),
    )(meta, u, zt, alog, dxp, ddt, dap, dbc, zb, sbin)


def run_leave(meta, du, ain, dgate, dz, nrm, wt, taps, width):
    inner, length = dgate.shape
    dm = nrm.shape[1]
    nb = length // BLK
    nk = BLK // (2 * width)
    wrows = wt.shape[0]
    rowsb = pl.BlockSpec((nk, width, dm), lambda j, *_: (j, 0, 0))
    colb = lambda n: pl.BlockSpec((n, BLK), lambda j, *_: (0, j))
    nblk = length // (2 * width)
    return pl.pallas_call(
        leave,
        grid_spec=pltpu.PrefetchScalarGridSpec(
            num_scalar_prefetch=1,
            grid=(nb,),
            in_specs=[
                colb(inner + 128),
                pl.BlockSpec((inner + 128, 128), lambda j, *_: (0, jnp.minimum(2 * j + 2, 2 * nb - 1))),
                colb(inner + 128),
                colb(inner),
                colb(ZR),
                pl.BlockSpec((BLK, dm), lambda j, *_: (j, 0)),
                full(wt.shape),
                full(taps.shape),
            ],
            out_specs=[rowsb, rowsb, full((dm, wrows)), full((4, inner + 128, 128))],
            scratch_shapes=[pltpu.VMEM((wrows, dm), F32), pltpu.VMEM((wrows, BLK), BF)],
        ),
        out_shape=[sds((nblk, width, dm), F32), sds((nblk, width, dm), BF), sds((dm, wrows), BF), sds((4, inner + 128, 128), F32)],
        compiler_params=_params(),
        cost_estimate=pl.CostEstimate(flops=4 * length * dm * wrows, bytes_accessed=30_000_000, transcendentals=0),
    )(meta, du, du, ain, dgate, dz, nrm, wt, taps)


def permute_slots(rows, sender):
    def body(order, src, dst):
        dst[...] = src[...]

    shape = (1,) + rows.shape[1:]
    zeros = (0,) * (rows.ndim - 1)
    return pl.pallas_call(
        body,
        grid_spec=pltpu.PrefetchScalarGridSpec(
            num_scalar_prefetch=1,
            grid=(rows.shape[0],),
            in_specs=[pl.BlockSpec(shape, lambda i, order: (order[i],) + zeros)],
            out_specs=pl.BlockSpec(shape, lambda i, order: (i,) + zeros),
        ),
        out_shape=sds(rows.shape, rows.dtype),
        compiler_params=_params(),
    )(sender, rows)


SWAP = [(0, 1), (1, 0)]
CORNER = [(0, 0), (1, 2), (2, 1), (3, 3)]


def twin(v, axis):
    return lax.ppermute(v, axis, SWAP)


def corner(v):
    return lax.ppermute(v, ("core", "tensor"), CORNER)


def both(v, other, index):
    return jnp.stack([jnp.where(index == 0, v, other), jnp.where(index == 0, other, v)])


def gather_weights(pack):
    n = lax.axis_size("z")
    z, x, y = (lax.axis_index(a) for a in ("z", "x", "tensor"))
    line = jnp.zeros((n,) + pack.shape, pack.dtype)
    line = lax.dynamic_update_index_in_dim(line, pack, z, 0)
    for k in range(1, n):
        got = lax.ppermute(pack, "z", [(i, (i + k) % n) for i in range(n)])
        line = lax.dynamic_update_index_in_dim(line, got, (z - k) % n, 0)
    mid = pack.shape[1] // 2
    a, b = line[..., :mid], line[..., mid:]
    a = both(a, twin(a, "x"), x)
    b = both(b, twin(b, "tensor"), y)
    a = both(a, twin(a, "tensor"), y)
    b = both(b, twin(b, "x"), x)
    a = jnp.transpose(a, (2, 1, 0, 3, 4))
    b = jnp.transpose(b, (2, 0, 1, 3, 4))
    return jnp.concatenate([a, b], -1)


def halve(v, axis, dim):
    i = lax.axis_index(axis)
    keep = lax.dynamic_index_in_dim(v, i, dim, False)
    send = lax.dynamic_index_in_dim(v, 1 - i, dim, False).astype(BF)
    return keep.astype(F32) + twin(send, axis).astype(F32)


def scatter_sum(v, cut):
    n = lax.axis_size("z")
    z = lax.axis_index("z")
    a = halve(halve(v[..., :cut], "x", 1).astype(BF), "tensor", 1)
    b = halve(halve(v[..., cut:], "tensor", 2).astype(BF), "x", 1)
    c = jnp.concatenate([a, b], -1)
    total = lax.dynamic_index_in_dim(c, z, 0, False)
    low = c.astype(BF)
    for k in range(1, n):
        send = lax.dynamic_index_in_dim(low, (z + k) % n, 0, False)
        total = total + lax.ppermute(send, "z", [(i, (i + k) % n) for i in range(n)]).astype(F32)
    return total


def total_of(v):
    for axis in ("x", "tensor"):
        v = v + twin(v, axis)
    n = lax.axis_size("z")
    k = 1
    while k < n:
        v = v + lax.ppermute(v, "z", [(i, i ^ k) for i in range(n)])
        k *= 2
    return v


def pad_rows(fwd, bwd):
    h = fwd.shape[0]
    gap = jnp.zeros((16 - h,) + fwd.shape[1:], fwd.dtype)
    return jnp.concatenate([fwd, gap, bwd, gap], 0)


def shards(
    layer_in,
    out_grad,
    seq_lengths,
    slot_perm,
    norm_gain,
    w_gate,
    w_inner,
    w_bc,
    w_dt,
    conv_x,
    conv_bc,
    dt_bias,
    a_log,
    dskip,
    inner_gain,
    w_out,
):
    z, x, core, y = (lax.axis_index(a) for a in ("z", "x", "core", "tensor"))
    nz = lax.axis_size("z")
    group = ("tensor", "z", "x")
    seqs, _, width, dm = layer_in.shape
    inner = w_gate.shape[1]
    heads = a_log.shape[0]
    rows = w_gate.shape[0]
    slot = lax.axis_index(group)
    ids = jnp.arange(seqs, dtype=jnp.int32)
    sender = jnp.sum(jnp.where(slot_perm[None, :] == ids[:, None], ids[None, :], 0), axis=1)
    my_length = jnp.sum(jnp.where(slot_perm == slot, seq_lengths, 0))
    meta = jnp.stack([core.astype(jnp.int32), my_length.astype(jnp.int32)])

    dt_cols = jnp.transpose(w_dt.reshape(rows, heads, 2), (0, 2, 1))
    dt_cols = jnp.pad(dt_cols, ((0, 0), (0, 0), (0, 16 - heads))).reshape(rows, ZR)
    pack = jnp.concatenate([w_out.T, w_gate, w_inner, w_bc, jnp.pad(dt_cols, ((0, 0), (0, 128 - ZR)))], 1)
    tiny = jnp.concatenate([dt_bias, a_log, dskip, jnp.zeros((inner - 4 * heads,), F32)])
    mine = corner(jnp.concatenate([conv_x, inner_gain[None], tiny[None], jnp.zeros((2, inner), F32)], 0))
    taps = jnp.concatenate([mine[0:4].T, conv_bc.T], 0)
    gain_u = mine[4][:, None]
    bias = mine[5, 0 : 2 * heads].reshape(heads, 2)
    alog = mine[5, 2 * heads : 3 * heads]
    skip = mine[5, 3 * heads : 4 * heads]
    bias = pad_rows(bias[:, 0:1], bias[:, 1:2])
    alog = pad_rows(alog[:, None], alog[:, None])

    rows_own = lax.all_to_all(permute_slots(layer_in[:, 0], sender), group, 0, 0, tiled=True)
    rows_oth = twin(rows_own, "core")
    weights = gather_weights(corner(pack)).reshape(dm, pack.shape[1])
    cot_own = lax.all_to_all(out_grad[:, 0], group, 0, 0, tiled=True)
    cot_oth = twin(cot_own, "core")

    nrm, gate, ain, u, zt, sf, wt = run_enter(meta, rows_own, rows_oth, weights, norm_gain[None], taps, bias, alog)
    own, oth, dgate, dxp, ddt, dap, dbc, zb, sbin, gwo, dgain, dsk = run_mix(
        meta, skip, cot_own, cot_oth, weights, gate, u, zt, sf, gain_u, alog
    )
    position = (2 * jnp.arange(rows_own.shape[0], dtype=jnp.int32)[:, None] + core) * width
    position = position + jnp.arange(width, dtype=jnp.int32)[None, :]
    mask = (position < my_length).astype(F32)[..., None]
    xf = rows_own.astype(F32)
    out_rows = xf + mask * (own + twin(oth, "core").astype(F32))
    output = lax.all_to_all(out_rows.astype(BF), group, 0, 0, tiled=True)
    gwo_sum = scatter_sum(gwo.reshape(nz, 2, 2, rows, inner), inner // 2)

    du, dz, dbias, dal = run_carry(meta, u, zt, alog, dxp, ddt, dap, dbc, zb, sbin)
    gown, goth, gw, dtaps = run_leave(meta, du, ain, dgate, dz, nrm, wt, taps, width)
    gn = gown + twin(goth, "core").astype(F32)
    inv = lax.rsqrt(jnp.mean(xf * xf, axis=-1, keepdims=True) + 1e-05)
    unit = xf * inv
    scaled = gn * norm_gain
    norm_part = jnp.sum(gn * unit, axis=(0, 1))
    back = cot_own.astype(F32) + inv * (scaled - unit * jnp.mean(scaled * unit, axis=-1, keepdims=True))
    input_grad = lax.all_to_all(back.astype(BF), group, 0, 0, tiled=True)

    gw_sum = scatter_sum(gw.reshape(nz, 2, 2, rows, gw.shape[1]), inner)
    bc_part = gw_sum[:, 2 * inner : 2 * inner + 128]
    bc_part = bc_part + twin(bc_part, "core")
    grads = corner(
        jnp.concatenate([gwo_sum, gw_sum[:, : 2 * inner], bc_part, gw_sum[:, 2 * inner + 128 :]], 1).astype(BF)
    ).astype(F32)
    out_sum = grads[:, :inner].T
    gate_sum = grads[:, inner : 2 * inner]
    inner_sum = grads[:, 2 * inner : 3 * inner]
    bc_sum = grads[:, 3 * inner : 3 * inner + 128]
    dt_sum = grads[:, 3 * inner + 128 :].reshape(rows, 2, 16)[:, :, :heads]
    dt_sum = jnp.transpose(dt_sum, (0, 2, 1)).reshape(rows, 2 * heads)

    dtap = jnp.sum(dtaps, axis=-1)
    dbias = jnp.sum(dbias, axis=1).reshape(2, 16)[:, :heads].T.reshape(2 * heads)
    dal = jnp.sum(dal, axis=1).reshape(2, 16)[:, :heads].sum(0)
    dskips = jnp.sum(dsk, axis=1)[:heads]
    half = [dtap[:, :inner].reshape(-1), jnp.sum(dgain, axis=1), dbias, dal, dskips]
    summed = [norm_part, dtap[:, inner:].reshape(-1)]
    sizes = [v.shape[0] for v in half + summed]
    vec = jnp.concatenate(half + summed)
    vec = total_of(jnp.pad(vec, (0, -vec.shape[0] % 1024)).reshape(-1, 128)).reshape(-1)
    pair = lax.ppermute(vec, "core", SWAP)
    here = jnp.where(core == y, vec, pair)
    joint = vec + pair
    cuts = [sum(sizes[:i]) for i in range(len(sizes) + 1)]
    convx_g, gain_g, bias_g, alog_g, skip_g = (here[cuts[i] : cuts[i + 1]] for i in range(5))
    norm_g, convbc_g = (joint[cuts[i] : cuts[i + 1]] for i in (5, 6))
    return (
        output[:, None],
        input_grad[:, None],
        norm_g,
        gate_sum,
        inner_sum,
        bc_sum,
        dt_sum,
        convx_g.reshape(4, inner),
        convbc_g.reshape(4, 128),
        bias_g,
        alog_g,
        skip_g,
        gain_g,
        out_sum,
    )


def solution(mesh):
    dp, tensor = mesh.devices.shape
    fine = Mesh(mesh.devices.reshape(dp // 4, 2, 2, tensor), ("z", "x", "core", "tensor"))
    d = ("z", "x", "core")
    t = "tensor"
    return jax.shard_map(
        shards,
        mesh=fine,
        in_specs=(
            P(None, t, d, None),
            P(None, t, d, None),
            P(),
            P(),
            P(),
            P(d, t),
            P(d, t),
            P(d, None),
            P(d, t),
            P(None, t),
            P(),
            P(t),
            P(t),
            P(t),
            P(t),
            P(t, d),
        ),
        out_specs=(
            P(None, t, d, None),
            P(None, t, d, None),
            P(),
            P(d, t),
            P(d, t),
            P(d, None),
            P(d, t),
            P(None, t),
            P(),
            P(t),
            P(t),
            P(t),
            P(t),
            P(t, d),
        ),
        check_vma=False,
    )
```

```python
import functools
import jax
import jax.numpy as jnp
from jax import lax
from jax.experimental import pallas as pl
from jax.experimental.pallas import tpu as pltpu
from jax.sharding import Mesh
from jax.sharding import PartitionSpec as P

F32 = jnp.float32
BF = jnp.bfloat16
CH = 128
BLK = 256
ZR = 32
MT = False
HIGH = lax.Precision.HIGHEST
VMEM_LIMIT = 60 * 1024 * 1024


def nn(a, b):
    return lax.dot_general(a, b, (((1,), (0,)), ((), ())), preferred_element_type=F32)


def nt(a, b):
    return lax.dot_general(a, b, (((1,), (1,)), ((), ())), preferred_element_type=F32)


def tn(a, b):
    return lax.dot_general(a, b, (((0,), (0,)), ((), ())), preferred_element_type=F32)


def running(rows, tri):
    return lax.dot_general(rows, tri, (((1,), (0,)), ((), ())), precision=HIGH, preferred_element_type=F32)


def softplus(z):
    return jnp.maximum(z, 0.0) + jnp.log1p(jnp.exp(-jnp.abs(z)))


def sigmoid(v):
    return 1.0 / (1.0 + jnp.exp(-v))


def tri(cond):
    r = lax.broadcasted_iota(jnp.int32, (CH, CH), 0)
    c = lax.broadcasted_iota(jnp.int32, (CH, CH), 1)
    return jnp.where(cond(r, c), 1.0, 0.0).astype(F32)


def interleave(core, a_ref, b_ref):
    parts = []
    for i in range(a_ref.shape[0]):
        a, b = a_ref[i].astype(F32), b_ref[i].astype(F32)
        parts += [jnp.where(core == 0, a, b), jnp.where(core == 0, b, a)]
    return jnp.concatenate(parts, 0)


def split_rows(core, v, own_ref, oth_ref):
    width = own_ref.shape[1]
    for i in range(own_ref.shape[0]):
        e = v[2 * i * width : (2 * i + 1) * width]
        o = v[(2 * i + 1) * width : (2 * i + 2) * width]
        own_ref[i] = jnp.where(core == 0, e, o).astype(own_ref.dtype)
        oth_ref[i] = jnp.where(core == 0, o, e).astype(oth_ref.dtype)


def decays(z, alog, mask):
    dt = softplus(z)
    a = -jnp.exp(alog) * dt
    cs = running(a, tri(lambda r, c: r <= c))
    return dt * mask, a, cs


def block_row(meta, k, dx, dy, sign):
    n = meta[5]
    z = lax.rem(meta[2] + sign * k + n, n)
    return (z * 2 + (meta[3] ^ dx)) * 2 + (meta[4] ^ dy)


def put_rows(w, meta, ref, first, count, dx, dy):
    if count == 0:
        w[...] = ref[...]
        return
    rows = ref.shape[1]
    for i in range(count):
        at = pl.multiple_of(block_row(meta, first + i, dx, dy, -1) * rows, 16)
        w[pl.ds(at, rows), :] = ref[i]


def enter(near, meta, xa, xb, *refs):
    pieces, refs = refs[: len(near)], refs[len(near) :]
    gain, taps, bias, alog, nrm, gate, ain, u, zt, sf, wt, wo, halo, state, vfe, w = refs
    j = pl.program_id(0)
    core, length = meta[0], meta[1]
    inner = gate.shape[0]
    heads = inner // 64
    cat = inner + 2 * 64
    top = inner

    @pl.when(j == 0)
    def _():
        for ref, (first, count, dx, dy) in zip(pieces, near):
            put_rows(w, meta, ref, first, count, dx, dy)
        wo[...] = w[:, 0:inner].T
        wt[0 : 2 * inner + 128, :] = w[:, inner : 3 * inner + 128].T
        wt[2 * inner + 128 : 2 * inner + 128 + ZR, :] = w[:, 3 * inner + 128 : 3 * inner + 256].T[0:ZR]
        halo[...] = jnp.zeros_like(halo)
        state[...] = jnp.zeros_like(state)

    x = interleave(core, xa, xb)
    r = lax.rsqrt(jnp.mean(x * x, axis=-1, keepdims=True) + 1e-05)
    normed = (x * r * gain[...]).astype(BF)
    nrm[...] = normed
    gate[...] = nt(wt[0:top, :], normed)
    for g in range(0, cat, 128):
        cur = nt(wt[top + g : top + g + 128, :], normed)
        full = jnp.concatenate([halo[g : g + 128, :], cur], 1)
        halo[g : g + 128, :] = cur[:, BLK - 128 :]
        ain[g : g + 128, :] = cur.astype(ain.dtype)
        t = taps[g : g + 128, :]
        acc = t[:, 3:4] * cur
        for k in (1, 2, 3):
            acc = acc + t[:, 3 - k : 4 - k] * pltpu.roll(full, k, 1)[:, 128:]
        u[g : g + 128, :] = acc
    z = nt(wt[top + cat : top + cat + ZR, :], normed) + bias[...]
    zt[...] = z
    for q in range(BLK // CH):
        lanes = slice(q * CH, (q + 1) * CH)
        pos = j * BLK + q * CH + lax.broadcasted_iota(jnp.int32, (1, CH), 1)
        mask = jnp.where(pos < length, 1.0, 0.0)
        mdt, a, cs = decays(z[:, lanes], alog[...], mask)
        tot = cs[:, CH - 1 : CH]
        wrow = mdt * jnp.exp(tot - cs)
        etot = jnp.exp(tot)
        bu = u[inner : inner + 64, lanes]
        bt = (bu * sigmoid(bu)).astype(BF)
        for h in range(heads):
            hs = slice(64 * h, 64 * h + 64)
            uh = u[hs, lanes]
            vfe[hs, :] = (uh * sigmoid(uh) * wrow[h : h + 1, :]).astype(BF)
        add = nt(vfe[...], bt)
        for h in range(heads):
            hs = slice(64 * h, 64 * h + 64)
            sf[q, hs, :] = state[hs, :].astype(sf.dtype)
            state[hs, :] = state[hs, :] * etot[h : h + 1, :] + add[hs, :]


def send_rows(meta, src, outs):
    if len(outs) == 1:
        outs[0][...] = src[...]
        return
    rows = outs[0].shape[2]
    ahead, behind = outs[0].shape[1], outs[2].shape[1]
    for other in range(2):
        for k in range(ahead):
            for ref, dx in ((outs[0], 1), (outs[1], 0)):
                at = pl.multiple_of(block_row(meta, k, dx, other, 1) * rows, 16)
                ref[other, k] = src[pl.ds(at, rows), :].astype(BF)
        for k in range(behind):
            for ref, dy in ((outs[2], 1), (outs[3], 0)):
                at = pl.multiple_of(block_row(meta, ahead + k, other, dy, 1) * rows, 16)
                ref[other, k] = src[pl.ds(at, rows), :].astype(BF)


def message_shapes(plan, dm, cols):
    if plan is None:
        return [sds((dm, cols), F32)]
    ahead, behind, rows = plan
    return [sds((2, n, rows, cols), BF) for n in (ahead, ahead, behind, behind)]


def mix(meta, dskip, dya, dyb, wo, gate, u, zt, sf, gain, alog, own, oth, dgate, dxp, ddt, dap, dbc, zb, sbin, dgain, dsk, *refs):
    *gwo, gacc, gy, ynt, yin, dv, dye, vfe, vbe, sb, dsf, rows, xs, yfs, ybs, dys, mls, mus, pds = refs
    i = pl.program_id(0)
    last = pl.num_programs(0) - 1
    j = last - i
    core, length = meta[0], meta[1]
    inner = gate.shape[0]
    heads = inner // 64

    @pl.when(i == 0)
    def _():
        gacc[...] = jnp.zeros_like(gacc)
        sb[...] = jnp.zeros_like(sb)
        dsf[...] = jnp.zeros_like(dsf)
        dgain[...] = jnp.zeros_like(dgain)
        dsk[...] = jnp.zeros_like(dsk)

    cot = interleave(core, dya, dyb)
    rowpos = j * BLK + lax.broadcasted_iota(jnp.int32, (BLK, 1), 0)
    cot = jnp.where(rowpos < length, cot, 0.0).astype(BF)
    gy[...] = nt(wo[...], cot).astype(BF).astype(F32)
    low = lax.broadcasted_iota(jnp.int32, (CH, CH), 0) > lax.broadcasted_iota(jnp.int32, (CH, CH), 1)
    up = lax.broadcasted_iota(jnp.int32, (CH, CH), 0) < lax.broadcasted_iota(jnp.int32, (CH, CH), 1)
    for q in reversed(range(BLK // CH)):
        lanes = slice(q * CH, (q + 1) * CH)
        pos = j * BLK + q * CH + lax.broadcasted_iota(jnp.int32, (1, CH), 1)
        mask = jnp.where(pos < length, 1.0, 0.0)
        mdt, a, cs = decays(zt[:, lanes], alog[...], mask)
        csf = cs[0:16]
        ecb = cs[16:32] - a[16:32]
        totf = cs[0:16, CH - 1 : CH]
        totb = cs[16:32, CH - 1 : CH]
        ccf = csf.T
        ccb = ecb.T
        ef = jnp.exp(csf)
        wf = jnp.exp(totf - csf)
        eb = jnp.exp(totb - ecb)
        wb = jnp.exp(ecb)
        etf = jnp.exp(totf)
        etb = jnp.exp(totb)
        bu = u[inner : inner + 64, lanes]
        cu = u[inner + 64 : inner + 128, lanes]
        bt = (bu * sigmoid(bu)).astype(BF)
        ct = (cu * sigmoid(cu)).astype(BF)
        gmat = tn(ct, bt)
        glow = jnp.where(low, gmat, 0.0)
        gup = jnp.where(up, gmat, 0.0)
        gmat = tn(bt, ct)
        tlow = jnp.where(up, gmat, 0.0)
        tup = jnp.where(low, gmat, 0.0)
        sbb = sb[...].astype(BF)
        sbin[q] = sbb
        dsb = dsf[...].astype(BF)
        yin[0:inner, :] = nn(sf[q], ct)
        yin[inner : 2 * inner, :] = nn(sbb, ct)
        dv[...] = nn(dsb, bt)
        for h in range(heads):
            hs = slice(64 * h, 64 * h + 64)
            h1 = slice(h, h + 1)
            uh = u[hs, lanes]
            x = uh * sigmoid(uh)
            xs[hs, :] = x
            mf = mdt[h : h + 1, :]
            mb = mdt[16 + h : 17 + h, :]
            vf16 = (x * mf).astype(BF)
            vb16 = (x * mb).astype(BF)
            pm = jnp.exp(jnp.where(low, ccf[:, h1] - csf[h1, :], ecb[h1, :] - ccb[:, h1]))
            ml = (pm * glow).astype(BF)
            mu = (pm * gup).astype(BF)
            mls[h] = ml
            mus[h] = mu
            pds[h] = pm * jnp.where(low, mf, mb)
            if MT:
                pt = jnp.exp(jnp.where(up, csf[h1, :] - ccf[:, h1], ccb[:, h1] - ecb[h1, :]))
                ml = (pt * tlow).astype(BF)
                mu = (pt * tup).astype(BF)
                yfs[hs, :] = nn(vf16, ml) + yin[hs, :] * ef[h1, :]
                ybs[hs, :] = nn(vb16, mu)
            else:
                yfs[hs, :] = nt(vf16, ml) + yin[hs, :] * ef[h1, :]
                ybs[hs, :] = nt(vb16, mu)
        for h in range(heads):
            hs = slice(64 * h, 64 * h + 64)
            h1 = slice(h, h + 1)
            x = xs[hs, :]
            ybi = yin[inner + 64 * h : inner + 64 * h + 64, :] * eb[h1, :]
            yf = yfs[hs, :]
            yb = ybs[hs, :] + ybi
            yt = yf + yb + dskip[h] * x
            gt = gate[hs, lanes]
            sg = sigmoid(gt)
            sl = gt * sg
            g = yt * sl
            ri = lax.rsqrt(jnp.mean(g * g, axis=0, keepdims=True) + 1e-05)
            gh = g * ri
            gn = gain[hs, :]
            ynt[hs, lanes] = (gh * gn).astype(BF)
            gyh = gy[hs, lanes]
            dgain[hs, :] += gyh * gh
            ds = gyh * gn
            dg = ri * (ds - gh * jnp.mean(ds * gh, axis=0, keepdims=True))
            dgate[hs, lanes] = (dg * yt * (sg * (1.0 + gt * (1.0 - sg)))).astype(BF)
            dy = dg * sl
            dyb16 = dy.astype(BF)
            dys[hs, :] = dyb16
            dyr = dyb16.astype(F32)
            rows[2, h1, :] = jnp.sum(dyr * yf, axis=0, keepdims=True)
            rows[3, h1, :] = -jnp.sum(dyr * yb, axis=0, keepdims=True)
            rows[5, h1, :] = jnp.sum(dyr * ybi, axis=0, keepdims=True)
            dsk[h1, :] += jnp.sum(dy * x, axis=0, keepdims=True)
            dxp[hs, lanes] = dskip[h] * dy
            dye[hs, :] = (dy * ef[h1, :]).astype(BF)
            dye[inner + 64 * h : inner + 64 * h + 64, :] = (dy * eb[h1, :]).astype(BF)
        dg_sum = jnp.zeros((CH, CH), F32)
        for h in range(heads):
            hs = slice(64 * h, 64 * h + 64)
            h1 = slice(h, h + 1)
            x = xs[hs, :]
            mf = mdt[h : h + 1, :]
            mb = mdt[16 + h : 17 + h, :]
            vf = x * mf
            vb = x * mb
            vfr = vf.astype(BF).astype(F32)
            dyb16 = dys[hs, :]
            dvi = dv[hs, :] * wf[h1, :]
            dvf = nn(dyb16, mls[h]) + dvi
            dvb = nn(dyb16, mus[h])
            dg_sum = dg_sum + tn(dyb16, x.astype(BF)) * pds[h]
            rows[0, h1, :] = jnp.sum(x * dvf, axis=0, keepdims=True)
            rows[1, h1, :] = jnp.sum(x * dvb, axis=0, keepdims=True)
            rows[2, h1, :] += -jnp.sum(vfr * dvf, axis=0, keepdims=True)
            rows[3, h1, :] += jnp.sum(vb.astype(BF).astype(F32) * dvb, axis=0, keepdims=True)
            prod = jnp.sum(dsf[hs, :] * sf[q, hs, :].astype(F32), axis=0, keepdims=True)
            prod = jnp.sum(prod, axis=1, keepdims=True) * etf[h1, :]
            rows[4, h1, :] = jnp.sum(vfr * dvi, axis=0, keepdims=True) + prod * (1.0 / CH)
            dxp[hs, lanes] += mf * dvf + mb * dvb
            vfe[hs, :] = (vf * wf[h1, :]).astype(BF)
            vbe[hs, :] = (vb * wb[h1, :]).astype(BF)
        dgb = jnp.where(low | up, dg_sum, 0.0).astype(BF)
        dbc[64:128, lanes] = nt(bt, dgb) + tn(sf[q], dye[0:inner, :]) + tn(sbb, dye[inner : 2 * inner, :])
        dbc[0:64, lanes] = nn(ct, dgb) + tn(dsb, vfe[...])
        grow = nt(dye[...], ct)
        srow = nt(vbe[...], bt)
        zb[q] = grow[inner : 2 * inner, :].astype(zb.dtype)
        for h in range(heads):
            hs = slice(64 * h, 64 * h + 64)
            dsf[hs, :] = dsf[hs, :] * etf[h : h + 1, :] + grow[hs, :]
            sb[hs, :] = sb[hs, :] * etb[h : h + 1, :] + srow[hs, :]
        ddt[0:16, lanes] = rows[0] * mask
        ddt[16:32, lanes] = rows[1] * mask
        dap[0:16, lanes] = running(rows[2], tri(lambda r, c: r >= c)) + jnp.sum(rows[4], axis=1, keepdims=True)
        dap[16:32, lanes] = running(rows[3], tri(lambda r, c: r > c)) + jnp.sum(rows[5], axis=1, keepdims=True)
    o = tn(ynt[...], wo[...])
    split_rows(core, o, own, oth)
    gacc[...] += nn(ynt[...], cot)

    @pl.when(i == last)
    def _():
        gacc[...] = gacc[...].T
        send_rows(meta, gacc, gwo)


def carry(meta, u, zt, alog, dxp, ddt, dap, dbc, zb, sbin, du, dz, dbias, dal, dsb, dvs, vbe, row):
    j = pl.program_id(0)
    length = meta[1]
    inner = dxp.shape[0]
    heads = inner // 64

    @pl.when(j == 0)
    def _():
        dsb[...] = jnp.zeros_like(dsb)
        dbias[...] = jnp.zeros_like(dbias)
        dal[...] = jnp.zeros_like(dal)
        row[...] = jnp.zeros_like(row)

    for q in range(BLK // CH):
        lanes = slice(q * CH, (q + 1) * CH)
        pos = j * BLK + q * CH + lax.broadcasted_iota(jnp.int32, (1, CH), 1)
        mask = jnp.where(pos < length, 1.0, 0.0)
        z = zt[:, lanes]
        mdt, a, cs = decays(z, alog[...], mask)
        ecb = cs[16:32] - a[16:32]
        etb = jnp.exp(cs[16:32, CH - 1 : CH])
        wb = jnp.exp(ecb)
        mw = mdt[16:32] * wb
        bu = u[inner : inner + 64, lanes]
        cu = u[inner + 64 : inner + 128, lanes]
        sgb = sigmoid(bu)
        sgc = sigmoid(cu)
        bt = (bu * sgb).astype(BF)
        dsb16 = dsb[...].astype(BF)
        dvs[...] = nn(dsb16, bt)
        for h in range(heads):
            hs = slice(64 * h, 64 * h + 64)
            h1 = slice(h, h + 1)
            uh = u[hs, lanes]
            sg = sigmoid(uh)
            x = uh * sg
            raw = dvs[hs, :]
            row[0, h1, :] = jnp.sum(x * raw, axis=0, keepdims=True) * wb[h1, :]
            prod = jnp.sum(dsb[hs, :] * sbin[q, hs, :].astype(F32), axis=0, keepdims=True)
            row[1, h1, :] = jnp.broadcast_to(jnp.sum(prod, axis=1, keepdims=True) * etb[h1, :], (1, CH))
            dx = dxp[hs, lanes] + raw * mw[h1, :]
            du[hs, lanes] = dx * (sg * (1.0 + uh * (1.0 - sg)))
            vbe[hs, :] = (x * mw[h1, :]).astype(BF)
        db = dbc[0:64, lanes] + tn(dsb16, vbe[...])
        du[inner : inner + 64, lanes] = db * (sgb * (1.0 + bu * (1.0 - sgb)))
        du[inner + 64 : inner + 128, lanes] = dbc[64:128, lanes] * (sgc * (1.0 + cu * (1.0 - sgc)))
        for h in range(heads):
            hs = slice(64 * h, 64 * h + 64)
            dsb[hs, :] = dsb[hs, :] * etb[h : h + 1, :] + zb[q, hs, :].astype(F32)
        dab = dap[16:32, lanes] + running(mdt[16:32] * row[0], tri(lambda r, c: r > c)) + row[1]
        da = jnp.concatenate([dap[0:16, lanes], dab], 0)
        dd = jnp.concatenate([ddt[0:16, lanes], ddt[16:32, lanes] + row[0] * mask], 0)
        dal[...] += da * a
        dzz = (dd - jnp.exp(alog[...]) * da) * sigmoid(z)
        dbias[...] += dzz
        dz[:, lanes] = dzz.astype(dz.dtype)


def lane_sums(v):
    ones = jnp.ones((8, v.shape[1]), F32)
    return lax.dot_general(ones, v, (((1,), (1,)), ((), ())), precision=HIGH, preferred_element_type=F32)[0:1]


def weigh(meta, du, nxt, ain, dgate, dz, nrm, taps, wt, gain, dgain, dbias, dal, dsk, cat, small, *refs):
    *gw, acc, flat, dtaps = refs
    j = pl.program_id(0)
    last = pl.num_programs(0) - 1
    inner = dgate.shape[0]
    conv = inner + 128

    @pl.when(j == 0)
    def _():
        dtaps[...] = jnp.zeros_like(dtaps)
        acc[...] = jnp.zeros_like(acc)

    cat[0:inner, :] = dgate[...]
    for g in range(0, conv, 128):
        cur = du[g : g + 128, :]
        after = jnp.where(j == last, 0.0, nxt[g : g + 128, :])
        full = jnp.concatenate([cur, after], 1)
        a = ain[g : g + 128, :].astype(F32)
        t = taps[g : g + 128, :]
        total = t[:, 3:4] * cur
        p = a * cur
        dtaps[3, g : g + 128, :] += p[:, 0:128] + p[:, 128:256]
        for k in (1, 2, 3):
            moved = pltpu.roll(full, BLK + 128 - k, 1)[:, 0:BLK]
            total = total + t[:, 3 - k : 4 - k] * moved
            p = a * moved
            dtaps[3 - k, g : g + 128, :] += p[:, 0:128] + p[:, 128:256]
        cat[inner + g : inner + g + 128, :] = total.astype(BF)
    cat[inner + conv : inner + conv + ZR, :] = dz[...]
    acc[...] += nn(cat[...], nrm[...])

    @pl.when(j == last)
    def _():
        flat[...] = acc[...].T
        send_rows(meta, flat, gw)
        small[...] = jnp.zeros_like(small)
        for k in range(4):
            small[k : k + 1, :] = lane_sums(dtaps[k])
        small[4:5, 0:inner] = lane_sums(dgain[...])
        norm = jnp.zeros((1, nrm.shape[1]), F32)
        for g in range(0, acc.shape[0], 32):
            norm = norm + jnp.sum(acc[g : g + 32, :] * wt[g : g + 32, :].astype(F32), axis=0, keepdims=True)
        small[5:6, 0:inner] = norm / gain[...]
        for i, ref in enumerate((dbias, dal, dsk)):
            small[6:7, 128 * i : 128 * i + ref.shape[0]] = lane_sums(ref[...])


def leave(meta, cat, wt, own, oth):
    gn = tn(cat[...], wt[...])
    split_rows(meta[0], gn, own, oth)


def _params():
    return pltpu.CompilerParams(dimension_semantics=("arbitrary",), vmem_limit_bytes=VMEM_LIMIT)


def full(shape):
    return pl.BlockSpec(shape, lambda j, *_: (0,) * len(shape))


def sds(shape, dt):
    return jax.ShapeDtypeStruct(shape, dt)


def run_enter(meta, xa, xb, pieces, near, gain, taps, bias, alog):
    nblk, width, dm = xa.shape
    length = 2 * nblk * width
    inner = taps.shape[0] - 128
    nk = BLK // (2 * width)
    nb = length // BLK
    rowsb = pl.BlockSpec((nk, width, dm), lambda j, *_: (j, 0, 0))
    colb = lambda n: pl.BlockSpec((n, BLK), lambda j, *_: (0, j))
    wrows = 2 * inner + 128 + ZR
    return pl.pallas_call(
        functools.partial(enter, near),
        grid_spec=pltpu.PrefetchScalarGridSpec(
            num_scalar_prefetch=1,
            grid=(nb,),
            in_specs=[rowsb, rowsb]
            + [full(p.shape) for p in pieces]
            + [full(gain.shape), full(taps.shape), full(bias.shape), full(alog.shape)],
            out_specs=[
                pl.BlockSpec((BLK, dm), lambda j, *_: (j, 0)),
                colb(inner),
                colb(inner + 128),
                colb(inner + 128),
                colb(ZR),
                pl.BlockSpec((BLK // CH, inner, 64), lambda j, *_: (j, 0, 0)),
                full((wrows, dm)),
                full((inner, dm)),
            ],
            scratch_shapes=[
                pltpu.VMEM((inner + 128, 128), F32),
                pltpu.VMEM((inner, 64), F32),
                pltpu.VMEM((inner, CH), BF),
                pltpu.VMEM((dm, pieces[0].shape[-1]), BF),
            ],
        ),
        out_shape=[
            sds((length, dm), BF),
            sds((inner, length), F32),
            sds((inner + 128, length), BF),
            sds((inner + 128, length), F32),
            sds((ZR, length), F32),
            sds((length // CH, inner, 64), BF),
            sds((wrows, dm), BF),
            sds((inner, dm), BF),
        ],
        compiler_params=_params(),
        cost_estimate=pl.CostEstimate(flops=2 * length * dm * wrows, bytes_accessed=30_000_000, transcendentals=4 * inner * length),
    )(meta, xa, xb, *pieces, gain, taps, bias, alog)


def run_mix(plan, meta, dskip, dya, dyb, wo, gate, u, zt, sf, gain, alog):
    nblk, width, dm = dya.shape
    length = 2 * nblk * width
    inner = gate.shape[0]
    nk = BLK // (2 * width)
    nb = length // BLK
    sent = message_shapes(plan, dm, inner)
    rowsb = pl.BlockSpec((nk, width, dm), lambda i, *_: (nb - 1 - i, 0, 0))
    colb = lambda n: pl.BlockSpec((n, BLK), lambda i, *_: (0, nb - 1 - i))
    stb = pl.BlockSpec((BLK // CH, inner, 64), lambda i, *_: (nb - 1 - i, 0, 0))
    return pl.pallas_call(
        mix,
        grid_spec=pltpu.PrefetchScalarGridSpec(
            num_scalar_prefetch=2,
            grid=(nb,),
            in_specs=[rowsb, rowsb, full((inner, dm)), colb(inner), colb(inner + 128), colb(ZR), stb, full(gain.shape), full(alog.shape)],
            out_specs=[
                rowsb,
                rowsb,
                colb(inner),
                colb(inner),
                colb(ZR),
                colb(ZR),
                colb(128),
                stb,
                stb,
                full((inner, CH)),
                full((16, CH)),
            ]
            + [full(m.shape) for m in sent],
            scratch_shapes=[
                pltpu.VMEM((inner, dm), F32),
                pltpu.VMEM((inner, BLK), F32),
                pltpu.VMEM((inner, BLK), BF),
                pltpu.VMEM((2 * inner, CH), F32),
                pltpu.VMEM((inner, CH), F32),
                pltpu.VMEM((2 * inner, CH), BF),
                pltpu.VMEM((inner, CH), BF),
                pltpu.VMEM((inner, CH), BF),
                pltpu.VMEM((inner, 64), F32),
                pltpu.VMEM((inner, 64), F32),
                pltpu.VMEM((6, 16, CH), F32),
                pltpu.VMEM((inner, CH), F32),
                pltpu.VMEM((inner, CH), F32),
                pltpu.VMEM((inner, CH), F32),
                pltpu.VMEM((inner, CH), BF),
                pltpu.VMEM((inner // 64, CH, CH), BF),
                pltpu.VMEM((inner // 64, CH, CH), BF),
                pltpu.VMEM((inner // 64, CH, CH), F32),
            ],
        ),
        out_shape=[
            sds((nblk, width, dm), F32),
            sds((nblk, width, dm), BF),
            sds((inner, length), BF),
            sds((inner, length), F32),
            sds((ZR, length), F32),
            sds((ZR, length), F32),
            sds((128, length), F32),
            sds((length // CH, inner, 64), BF),
            sds((length // CH, inner, 64), BF),
            sds((inner, CH), F32),
            sds((16, CH), F32),
        ]
        + sent,
        compiler_params=_params(),
        cost_estimate=pl.CostEstimate(flops=40 * 10**9, bytes_accessed=50_000_000, transcendentals=10**7),
    )(meta, dskip, dya, dyb, wo, gate, u, zt, sf, gain, alog)


def run_carry(meta, u, zt, alog, dxp, ddt, dap, dbc, zb, sbin):
    inner, length = dxp.shape
    nb = length // BLK
    colb = lambda n: pl.BlockSpec((n, BLK), lambda j, *_: (0, j))
    stb = pl.BlockSpec((BLK // CH, inner, 64), lambda j, *_: (j, 0, 0))
    return pl.pallas_call(
        carry,
        grid_spec=pltpu.PrefetchScalarGridSpec(
            num_scalar_prefetch=1,
            grid=(nb,),
            in_specs=[colb(inner + 128), colb(ZR), full(alog.shape), colb(inner), colb(ZR), colb(ZR), colb(128), stb, stb],
            out_specs=[colb(inner + 128), colb(ZR), full((ZR, CH)), full((ZR, CH))],
            scratch_shapes=[
                pltpu.VMEM((inner, 64), F32),
                pltpu.VMEM((inner, CH), F32),
                pltpu.VMEM((inner, CH), BF),
                pltpu.VMEM((2, 16, CH), F32),
            ],
        ),
        out_shape=[sds((inner + 128, length), F32), sds((ZR, length), BF), sds((ZR, CH), F32), sds((ZR, CH), F32)],
        compiler_params=_params(),
        cost_estimate=pl.CostEstimate(flops=10**9, bytes_accessed=30_000_000, transcendentals=10**6),
    )(meta, u, zt, alog, dxp, ddt, dap, dbc, zb, sbin)


def run_weigh(plan, meta, du, ain, dgate, dz, nrm, taps, *rest):
    inner, length = dgate.shape
    dm = nrm.shape[1]
    nb = length // BLK
    wrows = 2 * inner + 128 + ZR
    sent = message_shapes(plan, dm, wrows)
    colb = lambda n: pl.BlockSpec((n, BLK), lambda j, *_: (0, j))
    return pl.pallas_call(
        weigh,
        grid_spec=pltpu.PrefetchScalarGridSpec(
            num_scalar_prefetch=1,
            grid=(nb,),
            in_specs=[
                colb(inner + 128),
                pl.BlockSpec((inner + 128, 128), lambda j, *_: (0, jnp.minimum(2 * j + 2, 2 * nb - 1))),
                colb(inner + 128),
                colb(inner),
                colb(ZR),
                pl.BlockSpec((BLK, dm), lambda j, *_: (j, 0)),
                full(taps.shape),
            ]
            + [full(r.shape) for r in rest],
            out_specs=[colb(wrows), full((8, inner + 128))] + [full(m.shape) for m in sent],
            scratch_shapes=[
                pltpu.VMEM((wrows, dm), F32),
                pltpu.VMEM((dm, wrows), F32),
                pltpu.VMEM((4, inner + 128, 128), F32),
            ],
        ),
        out_shape=[sds((wrows, length), BF), sds((8, inner + 128), F32)] + sent,
        compiler_params=_params(),
        cost_estimate=pl.CostEstimate(flops=2 * length * dm * wrows, bytes_accessed=30_000_000, transcendentals=0),
    )(meta, du, du, ain, dgate, dz, nrm, taps, *rest)


def run_leave(meta, cat, wt, width):
    wrows, length = cat.shape
    dm = wt.shape[1]
    nk = BLK // (2 * width)
    nblk = length // (2 * width)
    rowsb = pl.BlockSpec((nk, width, dm), lambda j, *_: (j, 0, 0))
    return pl.pallas_call(
        leave,
        grid_spec=pltpu.PrefetchScalarGridSpec(
            num_scalar_prefetch=1,
            grid=(length // BLK,),
            in_specs=[
                pl.BlockSpec((wrows, BLK), lambda j, *_: (0, j)),
                full(wt.shape),
            ],
            out_specs=[rowsb, rowsb],
        ),
        out_shape=[sds((nblk, width, dm), F32), sds((nblk, width, dm), BF)],
        compiler_params=_params(),
        cost_estimate=pl.CostEstimate(flops=10**6, bytes_accessed=20_000_000, transcendentals=0),
    )(meta, cat, wt)


def permute_slots(rows, sender):
    def body(order, src, dst):
        for i in range(rows.shape[0]):
            dst[i] = src[order[i]]

    return pl.pallas_call(
        body,
        grid_spec=pltpu.PrefetchScalarGridSpec(
            num_scalar_prefetch=1, grid=(1,), in_specs=[full(rows.shape)], out_specs=full(rows.shape)
        ),
        out_shape=sds(rows.shape, rows.dtype),
        compiler_params=_params(),
    )(sender, rows)


WIDE = 60 * 10**9
SWAP = [(0, 1), (1, 0)]
CORNER = [(0, 0), (1, 2), (2, 1), (3, 3)]


def twin(v, axis):
    return lax.ppermute(v, axis, SWAP)


def corner(v):
    return lax.ppermute(v, ("core", "tensor"), CORNER)


def after(v, *others, wide=False):
    def body(*refs):
        pass

    space = pl.BlockSpec(memory_space=pl.ANY)
    return pl.pallas_call(
        body,
        in_specs=[space] * (1 + len(others)),
        out_specs=space,
        out_shape=sds(v.shape, v.dtype),
        input_output_aliases={0: 0},
        cost_estimate=pl.CostEstimate(flops=WIDE if wide else 0, bytes_accessed=0, transcendentals=0),
    )(v, *others)


def ahead_of(n, k):
    return [(i, (i + k) % n) for i in range(n)]


def gather_weights(pack, plan, moved):
    if plan is None:
        return [lax.all_gather(pack, ("z", "x", "tensor"), tiled=True)], [(0, 0, 0, 0)], moved, []
    ahead, behind, _ = plan
    got = [pack] + [lax.ppermute(pack, "z", ahead_of(ahead + behind, k)) for k in range(1, ahead + behind)]
    moved = after(moved, *got[1:])
    a, b = jnp.stack(got[:ahead]), jnp.stack(got[ahead:])
    a = after(a, moved, b, wide=True)
    b = after(b, a)
    both = [(i, 3 - i) for i in range(4)]
    by, bx, bxy = twin(b, "tensor"), twin(b, "x"), lax.ppermute(b, ("x", "tensor"), both)
    ax, ay, axy = twin(a, "x"), twin(a, "tensor"), lax.ppermute(a, ("x", "tensor"), both)
    near = [(0, ahead, 0, 0), (0, ahead, 1, 0), (0, ahead, 0, 1), (0, ahead, 1, 1)]
    far = [(ahead, behind, 0, 0), (ahead, behind, 0, 1), (ahead, behind, 1, 0), (ahead, behind, 1, 1)]
    return [a, ax, ay, axy, b, by, bx, bxy], near + far, moved, [ax, ay, axy, by, bx, bxy]


def add(kept, got):
    return kept.astype(F32) + got.astype(F32)


class ChipSum:
    def __init__(self, sent, plan):
        self.now, self.plan, self.got = sent, plan, []

    def send(self, step):
        s = self.now
        if self.plan is None:
            if step == 2:
                self.got = [lax.psum_scatter(s[0], ("z", "x", "tensor"), scatter_dimension=0, tiled=True)]
        elif step == 0:
            self.got = [twin(s[0], "x"), twin(s[2], "tensor")]
        elif step == 1:
            self.got = [twin(s[1], "tensor"), twin(s[3], "x")]
        else:
            n = len(s)
            self.got = [lax.ppermute(s[k], "z", ahead_of(n, k)) for k in range(1, n)]

    def hold(self, v):
        if self.plan is not None:
            at = 1 if len(self.now) == 4 and self.now[1].ndim == 4 else 0
            for i in (at, at + 2):
                self.now[i] = after(self.now[i], v)

    def add(self, step):
        s, g = self.now, self.got
        self.got = []
        if self.plan is None:
            self.now = g if step == 2 else s
        elif step == 0:
            a, b = add(s[1], g[0]), add(s[3], g[1])
            self.now = [a[0], a[1].astype(BF), b[0], b[1].astype(BF)]
        elif step == 1:
            a, b = add(s[0], g[0]), add(s[2], g[1])
            low = [a[k].astype(BF) for k in range(1, a.shape[0])] + [b[k].astype(BF) for k in range(b.shape[0])]
            self.now = [a[0]] + low
        else:
            total = s[0]
            for piece in g:
                total = add(total, piece)
            self.now = [total]


def pad_rows(fwd, bwd):
    h = fwd.shape[0]
    gap = jnp.zeros((16 - h,) + fwd.shape[1:], fwd.dtype)
    return jnp.concatenate([fwd, gap, bwd, gap], 0)


def shards(
    layer_in,
    out_grad,
    seq_lengths,
    slot_perm,
    norm_gain,
    w_gate,
    w_inner,
    w_bc,
    w_dt,
    conv_x,
    conv_bc,
    dt_bias,
    a_log,
    dskip,
    inner_gain,
    w_out,
):
    z, x, core, y = (lax.axis_index(a) for a in ("z", "x", "core", "tensor"))
    nz = lax.axis_size("z")
    group = ("tensor", "z", "x")
    seqs, _, width, dm = layer_in.shape
    inner = w_gate.shape[1]
    heads = a_log.shape[0]
    rows = w_gate.shape[0]
    slot = lax.axis_index(group)
    ids = jnp.arange(seqs, dtype=jnp.int32)
    sender = jnp.sum(jnp.where(slot_perm[None, :] == ids[:, None], ids[None, :], 0), axis=1)
    my_length = jnp.sum(jnp.where(slot_perm == slot, seq_lengths, 0))
    meta = jnp.stack([core, my_length, z, x, y, jnp.int32(nz)]).astype(jnp.int32)

    dt_cols = jnp.transpose(w_dt.reshape(rows, heads, 2), (0, 2, 1))
    dt_cols = jnp.pad(dt_cols, ((0, 0), (0, 0), (0, 16 - heads))).reshape(rows, ZR)
    pack = jnp.concatenate([w_out.T, w_gate, w_inner, w_bc, jnp.pad(dt_cols, ((0, 0), (0, 128 - ZR)))], 1)
    tiny = jnp.concatenate([dt_bias, a_log, dskip, jnp.zeros((inner - 4 * heads,), F32)])
    mine = corner(jnp.concatenate([conv_x, inner_gain[None], tiny[None], jnp.zeros((2, inner), F32)], 0))
    taps = jnp.concatenate([mine[0:4].T, conv_bc.T], 0)
    gain_u = mine[4][:, None]
    bias = mine[5, 0 : 2 * heads].reshape(heads, 2)
    alog = mine[5, 2 * heads : 3 * heads]
    skip = mine[5, 3 * heads : 4 * heads]
    bias = pad_rows(bias[:, 0:1], bias[:, 1:2])
    alog = pad_rows(alog[:, None], alog[:, None])

    ahead = nz // 2
    plan = (ahead, nz - ahead, rows) if rows % 16 == 0 else None
    moved = permute_slots(layer_in[:, 0], sender)
    pieces, near, moved, early = gather_weights(corner(pack), plan, moved)
    rows_own = lax.all_to_all(moved, group, 0, 0, tiled=True)
    dy = after(out_grad[:, 0], *early)
    rows_own = after(rows_own, *early)
    rows_oth = twin(rows_own, "core")
    cot_own = lax.all_to_all(dy, group, 0, 0, tiled=True)

    nrm, gate, ain, u, zt, sf, wt, wo = run_enter(meta, rows_own, rows_oth, pieces, near, norm_gain[None], taps, bias, alog)
    cot_own = after(cot_own, zt)
    cot_oth = twin(cot_own, "core")
    own, oth, dgate, dxp, ddt, dap, dbc, zb, sbin, dgain, dsk, *gwo = run_mix(
        plan, meta, skip, cot_own, cot_oth, wo, gate, u, zt, sf, gain_u, alog
    )
    position = (2 * jnp.arange(rows_own.shape[0], dtype=jnp.int32)[:, None] + core) * width
    position = position + jnp.arange(width, dtype=jnp.int32)[None, :]
    mask = (position < my_length).astype(F32)[..., None]
    xf = rows_own.astype(F32)
    oth = twin(oth, "core")
    out_grads = ChipSum(gwo, plan)
    out_grads.send(0)
    du, dz, dbias, dal = run_carry(meta, u, zt, alog, after(dxp, own, wide=True), ddt, dap, dbc, zb, sbin)
    out_rows = (xf + mask * add(after(own, du), oth)).astype(BF)
    output = lax.all_to_all(out_rows, group, 0, 0, tiled=True)
    out_grads.hold(out_rows)
    out_grads.add(0)
    out_grads.send(1)
    du = after(du, out_rows, wide=True)
    cat, small, *gw = run_weigh(
        plan, meta, du, ain, dgate, dz, nrm, taps, wt, norm_gain[None], dgain, dbias, dal, dsk
    )
    grads_in = ChipSum(gw, plan)
    grads_in.send(0)
    got = twin(small, "x")
    gown, goth = run_leave(meta, after(cat, small, wide=True), wt, width)

    gn = add(gown, twin(goth, "core"))
    inv = lax.rsqrt(jnp.mean(xf * xf, axis=-1, keepdims=True) + 1e-05)
    unit = xf * inv
    scaled = gn * norm_gain
    back = cot_own.astype(F32) + inv * (scaled - unit * jnp.mean(scaled * unit, axis=-1, keepdims=True))
    back = back.astype(BF)
    input_grad = lax.all_to_all(after(back, output), group, 0, 0, tiled=True)
    small = after(small, back) + got
    small = small + twin(small, "tensor")
    grads_in.hold(back)
    grads_in.add(0)
    grads_in.send(1)
    out_grads.hold(back)
    out_grads.add(1)
    out_grads.send(2)
    out_grads.add(2)
    k = 1
    while k < nz:
        small = small + lax.ppermute(small, "z", [(i, i ^ k) for i in range(nz)])
        k *= 2
    pair = twin(small, "core")
    grads_in.add(1)
    if plan is not None:
        grads_in.now = [after(v, input_grad) for v in grads_in.now]
    grads_in.send(2)
    grads_in.add(2)
    gw_sum, gwo_sum = grads_in.now[0], out_grads.now[0]

    bc_part = gw_sum[:, 2 * inner : 2 * inner + 128]
    bc_part = bc_part + twin(bc_part, "core")
    grads = jnp.concatenate([gwo_sum, gw_sum[:, : 2 * inner], bc_part, gw_sum[:, 2 * inner + 128 :]], 1)
    grads = corner(grads.astype(BF)).astype(F32)
    out_sum = grads[:, :inner].T
    gate_sum = grads[:, inner : 2 * inner]
    inner_sum = grads[:, 2 * inner : 3 * inner]
    bc_sum = grads[:, 3 * inner : 3 * inner + 128]
    dt_sum = grads[:, 3 * inner + 128 :].reshape(rows, 2, 16)[:, :, :heads]
    dt_sum = jnp.transpose(dt_sum, (0, 2, 1)).reshape(rows, 2 * heads)

    here = jnp.where(core == y, small, pair)
    joint = small + pair
    heads_of = lambda at: here[6, at : at + ZR].reshape(2, 16)[:, :heads]
    return (
        output[:, None],
        input_grad[:, None],
        joint[5, :inner],
        gate_sum,
        inner_sum,
        bc_sum,
        dt_sum,
        here[0:4, :inner],
        joint[0:4, inner:],
        heads_of(0).T.reshape(2 * heads),
        heads_of(128).sum(0),
        here[6, 256 : 256 + heads],
        here[4, :inner],
        out_sum,
    )


def solution(mesh):
    dp, tensor = mesh.devices.shape
    fine = Mesh(mesh.devices.reshape(dp // 4, 2, 2, tensor), ("z", "x", "core", "tensor"))
    d = ("z", "x", "core")
    t = "tensor"
    return jax.shard_map(
        shards,
        mesh=fine,
        in_specs=(
            P(None, t, d, None),
            P(None, t, d, None),
            P(),
            P(),
            P(),
            P(d, t),
            P(d, t),
            P(d, None),
            P(d, t),
            P(None, t),
            P(),
            P(t),
            P(t),
            P(t),
            P(t),
            P(t, d),
        ),
        out_specs=(
            P(None, t, d, None),
            P(None, t, d, None),
            P(),
            P(d, t),
            P(d, t),
            P(d, None),
            P(d, t),
            P(None, t),
            P(),
            P(t),
            P(t),
            P(t),
            P(t),
            P(t, d),
        ),
        check_vma=False,
    )
```

```python
import functools
import jax
import jax.numpy as jnp
from jax import lax
from jax.experimental import pallas as pl
from jax.experimental.pallas import tpu as pltpu
from jax.sharding import Mesh
from jax.sharding import PartitionSpec as P

F32 = jnp.float32
BF = jnp.bfloat16
CH = 128
BLK = 256
ZR = 32
MT = False
HIGH = lax.Precision.HIGHEST
VMEM_LIMIT = 60 * 1024 * 1024


def nn(a, b):
    return lax.dot_general(a, b, (((1,), (0,)), ((), ())), preferred_element_type=F32)


def nt(a, b):
    return lax.dot_general(a, b, (((1,), (1,)), ((), ())), preferred_element_type=F32)


def tn(a, b):
    return lax.dot_general(a, b, (((0,), (0,)), ((), ())), preferred_element_type=F32)


def running(rows, tri):
    return lax.dot_general(rows, tri, (((1,), (0,)), ((), ())), precision=HIGH, preferred_element_type=F32)


def softplus(z):
    return jnp.maximum(z, 0.0) + jnp.log1p(jnp.exp(-jnp.abs(z)))


def sigmoid(v):
    return 1.0 / (1.0 + jnp.exp(-v))


def tri(cond):
    r = lax.broadcasted_iota(jnp.int32, (CH, CH), 0)
    c = lax.broadcasted_iota(jnp.int32, (CH, CH), 1)
    return jnp.where(cond(r, c), 1.0, 0.0).astype(F32)


def interleave(core, a_ref, b_ref):
    parts = []
    for i in range(a_ref.shape[0]):
        a, b = a_ref[i].astype(F32), b_ref[i].astype(F32)
        parts += [jnp.where(core == 0, a, b), jnp.where(core == 0, b, a)]
    return jnp.concatenate(parts, 0)


def split_rows(core, v, own_ref, oth_ref):
    width = own_ref.shape[1]
    for i in range(own_ref.shape[0]):
        e = v[2 * i * width : (2 * i + 1) * width]
        o = v[(2 * i + 1) * width : (2 * i + 2) * width]
        own_ref[i] = jnp.where(core == 0, e, o).astype(own_ref.dtype)
        oth_ref[i] = jnp.where(core == 0, o, e).astype(oth_ref.dtype)


def decays(z, alog, mask):
    dt = softplus(z)
    a = -jnp.exp(alog) * dt
    cs = running(a, tri(lambda r, c: r <= c))
    return dt * mask, a, cs


def block_row(meta, k, dx, dy, sign):
    n = meta[5]
    z = lax.rem(meta[2] + sign * k + n, n)
    return (z * 2 + (meta[3] ^ dx)) * 2 + (meta[4] ^ dy)


def put_rows(w, meta, ref, first, count, dx, dy):
    if count == 0:
        w[...] = ref[...]
        return
    rows = ref.shape[1]
    for i in range(count):
        at = pl.multiple_of(block_row(meta, first + i, dx, dy, -1) * rows, 16)
        w[pl.ds(at, rows), :] = ref[i]


def enter(near, meta, xa, xb, *refs):
    pieces, refs = refs[: len(near)], refs[len(near) :]
    gain, taps, bias, alog, nrm, gate, ain, u, zt, sf, wt, wo, halo, state, vfe, w = refs
    j = pl.program_id(0)
    core, length = meta[0], meta[1]
    inner = gate.shape[0]
    heads = inner // 64
    cat = inner + 2 * 64
    top = inner

    @pl.when(j == 0)
    def _():
        for ref, (first, count, dx, dy) in zip(pieces, near):
            put_rows(w, meta, ref, first, count, dx, dy)
        wo[...] = w[:, 0:inner].T
        wt[0 : 2 * inner + 128, :] = w[:, inner : 3 * inner + 128].T
        wt[2 * inner + 128 : 2 * inner + 128 + ZR, :] = w[:, 3 * inner + 128 : 3 * inner + 256].T[0:ZR]
        halo[...] = jnp.zeros_like(halo)
        state[...] = jnp.zeros_like(state)

    x = interleave(core, xa, xb)
    r = lax.rsqrt(jnp.mean(x * x, axis=-1, keepdims=True) + 1e-05)
    normed = (x * r * gain[...]).astype(BF)
    nrm[...] = normed
    gate[...] = nt(wt[0:top, :], normed)
    for g in range(0, cat, 128):
        cur = nt(wt[top + g : top + g + 128, :], normed)
        full = jnp.concatenate([halo[g : g + 128, :], cur], 1)
        halo[g : g + 128, :] = cur[:, BLK - 128 :]
        ain[g : g + 128, :] = cur.astype(ain.dtype)
        t = taps[g : g + 128, :]
        acc = t[:, 3:4] * cur
        for k in (1, 2, 3):
            acc = acc + t[:, 3 - k : 4 - k] * pltpu.roll(full, k, 1)[:, 128:]
        u[g : g + 128, :] = acc
    z = nt(wt[top + cat : top + cat + ZR, :], normed) + bias[...]
    zt[...] = z
    for q in range(BLK // CH):
        lanes = slice(q * CH, (q + 1) * CH)
        pos = j * BLK + q * CH + lax.broadcasted_iota(jnp.int32, (1, CH), 1)
        mask = jnp.where(pos < length, 1.0, 0.0)
        mdt, a, cs = decays(z[:, lanes], alog[...], mask)
        tot = cs[:, CH - 1 : CH]
        wrow = mdt * jnp.exp(tot - cs)
        etot = jnp.exp(tot)
        bu = u[inner : inner + 64, lanes]
        bt = (bu * sigmoid(bu)).astype(BF)
        for h in range(heads):
            hs = slice(64 * h, 64 * h + 64)
            uh = u[hs, lanes]
            vfe[hs, :] = (uh * sigmoid(uh) * wrow[h : h + 1, :]).astype(BF)
        add = nt(vfe[...], bt)
        for h in range(heads):
            hs = slice(64 * h, 64 * h + 64)
            sf[q, hs, :] = state[hs, :].astype(sf.dtype)
            state[hs, :] = state[hs, :] * etot[h : h + 1, :] + add[hs, :]


def send_rows(meta, src, outs):
    if len(outs) == 1:
        outs[0][...] = src[...]
        return
    rows = outs[0].shape[2]
    ahead, behind = outs[0].shape[1], outs[2].shape[1]
    for other in range(2):
        for k in range(ahead):
            for ref, dx in ((outs[0], 1), (outs[1], 0)):
                at = pl.multiple_of(block_row(meta, k, dx, other, 1) * rows, 16)
                ref[other, k] = src[pl.ds(at, rows), :].astype(BF)
        for k in range(behind):
            for ref, dy in ((outs[2], 1), (outs[3], 0)):
                at = pl.multiple_of(block_row(meta, ahead + k, other, dy, 1) * rows, 16)
                ref[other, k] = src[pl.ds(at, rows), :].astype(BF)


def message_shapes(plan, dm, cols):
    if plan is None:
        return [sds((dm, cols), F32)]
    ahead, behind, rows = plan
    return [sds((2, n, rows, cols), BF) for n in (ahead, ahead, behind, behind)]


def mix(meta, dskip, dya, dyb, wo, gate, u, zt, sf, gain, alog, own, oth, dgate, dxp, ddt, dap, dbc, zb, sbin, dgain, dsk, *refs):
    *gwo, gacc, gy, ynt, yin, dv, dye, vfe, vbe, sb, dsf, rows, xs, yfs, ybs, dys, mls, mus, pds = refs
    i = pl.program_id(0)
    last = pl.num_programs(0) - 1
    j = last - i
    core, length = meta[0], meta[1]
    inner = gate.shape[0]
    heads = inner // 64

    @pl.when(i == 0)
    def _():
        gacc[...] = jnp.zeros_like(gacc)
        sb[...] = jnp.zeros_like(sb)
        dsf[...] = jnp.zeros_like(dsf)
        dgain[...] = jnp.zeros_like(dgain)
        dsk[...] = jnp.zeros_like(dsk)

    cot = interleave(core, dya, dyb)
    rowpos = j * BLK + lax.broadcasted_iota(jnp.int32, (BLK, 1), 0)
    cot = jnp.where(rowpos < length, cot, 0.0).astype(BF)
    gy[...] = nt(wo[...], cot).astype(BF).astype(F32)
    low = lax.broadcasted_iota(jnp.int32, (CH, CH), 0) > lax.broadcasted_iota(jnp.int32, (CH, CH), 1)
    up = lax.broadcasted_iota(jnp.int32, (CH, CH), 0) < lax.broadcasted_iota(jnp.int32, (CH, CH), 1)
    for q in reversed(range(BLK // CH)):
        lanes = slice(q * CH, (q + 1) * CH)
        pos = j * BLK + q * CH + lax.broadcasted_iota(jnp.int32, (1, CH), 1)
        mask = jnp.where(pos < length, 1.0, 0.0)
        mdt, a, cs = decays(zt[:, lanes], alog[...], mask)
        csf = cs[0:16]
        ecb = cs[16:32] - a[16:32]
        totf = cs[0:16, CH - 1 : CH]
        totb = cs[16:32, CH - 1 : CH]
        ccf = csf.T
        ccb = ecb.T
        ef = jnp.exp(csf)
        wf = jnp.exp(totf - csf)
        eb = jnp.exp(totb - ecb)
        wb = jnp.exp(ecb)
        etf = jnp.exp(totf)
        etb = jnp.exp(totb)
        bu = u[inner : inner + 64, lanes]
        cu = u[inner + 64 : inner + 128, lanes]
        bt = (bu * sigmoid(bu)).astype(BF)
        ct = (cu * sigmoid(cu)).astype(BF)
        gmat = tn(ct, bt)
        glow = jnp.where(low, gmat, 0.0)
        gup = jnp.where(up, gmat, 0.0)
        gmat = tn(bt, ct)
        tlow = jnp.where(up, gmat, 0.0)
        tup = jnp.where(low, gmat, 0.0)
        sbb = sb[...].astype(BF)
        sbin[q] = sbb
        dsb = dsf[...].astype(BF)
        yin[0:inner, :] = nn(sf[q], ct)
        yin[inner : 2 * inner, :] = nn(sbb, ct)
        dv[...] = nn(dsb, bt)
        for h in range(heads):
            hs = slice(64 * h, 64 * h + 64)
            h1 = slice(h, h + 1)
            uh = u[hs, lanes]
            x = uh * sigmoid(uh)
            xs[hs, :] = x
            mf = mdt[h : h + 1, :]
            mb = mdt[16 + h : 17 + h, :]
            vf16 = (x * mf).astype(BF)
            vb16 = (x * mb).astype(BF)
            pm = jnp.exp(jnp.where(low, ccf[:, h1] - csf[h1, :], ecb[h1, :] - ccb[:, h1]))
            ml = (pm * glow).astype(BF)
            mu = (pm * gup).astype(BF)
            mls[h] = ml
            mus[h] = mu
            pds[h] = pm * jnp.where(low, mf, mb)
            if MT:
                pt = jnp.exp(jnp.where(up, csf[h1, :] - ccf[:, h1], ccb[:, h1] - ecb[h1, :]))
                ml = (pt * tlow).astype(BF)
                mu = (pt * tup).astype(BF)
                yfs[hs, :] = nn(vf16, ml) + yin[hs, :] * ef[h1, :]
                ybs[hs, :] = nn(vb16, mu)
            else:
                yfs[hs, :] = nt(vf16, ml) + yin[hs, :] * ef[h1, :]
                ybs[hs, :] = nt(vb16, mu)
        for h in range(heads):
            hs = slice(64 * h, 64 * h + 64)
            h1 = slice(h, h + 1)
            x = xs[hs, :]
            ybi = yin[inner + 64 * h : inner + 64 * h + 64, :] * eb[h1, :]
            yf = yfs[hs, :]
            yb = ybs[hs, :] + ybi
            yt = yf + yb + dskip[h] * x
            gt = gate[hs, lanes]
            sg = sigmoid(gt)
            sl = gt * sg
            g = yt * sl
            ri = lax.rsqrt(jnp.mean(g * g, axis=0, keepdims=True) + 1e-05)
            gh = g * ri
            gn = gain[hs, :]
            ynt[hs, lanes] = (gh * gn).astype(BF)
            gyh = gy[hs, lanes]
            dgain[hs, :] += gyh * gh
            ds = gyh * gn
            dg = ri * (ds - gh * jnp.mean(ds * gh, axis=0, keepdims=True))
            dgate[hs, lanes] = (dg * yt * (sg * (1.0 + gt * (1.0 - sg)))).astype(BF)
            dy = dg * sl
            dyb16 = dy.astype(BF)
            dys[hs, :] = dyb16
            dyr = dyb16.astype(F32)
            rows[2, h1, :] = jnp.sum(dyr * yf, axis=0, keepdims=True)
            rows[3, h1, :] = -jnp.sum(dyr * yb, axis=0, keepdims=True)
            rows[5, h1, :] = jnp.sum(dyr * ybi, axis=0, keepdims=True)
            dsk[h1, :] += jnp.sum(dy * x, axis=0, keepdims=True)
            dxp[hs, lanes] = dskip[h] * dy
            dye[hs, :] = (dy * ef[h1, :]).astype(BF)
            dye[inner + 64 * h : inner + 64 * h + 64, :] = (dy * eb[h1, :]).astype(BF)
        dg_sum = jnp.zeros((CH, CH), F32)
        for h in range(heads):
            hs = slice(64 * h, 64 * h + 64)
            h1 = slice(h, h + 1)
            x = xs[hs, :]
            mf = mdt[h : h + 1, :]
            mb = mdt[16 + h : 17 + h, :]
            vf = x * mf
            vb = x * mb
            vfr = vf.astype(BF).astype(F32)
            dyb16 = dys[hs, :]
            dvi = dv[hs, :] * wf[h1, :]
            dvf = nn(dyb16, mls[h]) + dvi
            dvb = nn(dyb16, mus[h])
            dg_sum = dg_sum + tn(dyb16, x.astype(BF)) * pds[h]
            rows[0, h1, :] = jnp.sum(x * dvf, axis=0, keepdims=True)
            rows[1, h1, :] = jnp.sum(x * dvb, axis=0, keepdims=True)
            rows[2, h1, :] += -jnp.sum(vfr * dvf, axis=0, keepdims=True)
            rows[3, h1, :] += jnp.sum(vb.astype(BF).astype(F32) * dvb, axis=0, keepdims=True)
            prod = jnp.sum(dsf[hs, :] * sf[q, hs, :].astype(F32), axis=0, keepdims=True)
            prod = jnp.sum(prod, axis=1, keepdims=True) * etf[h1, :]
            rows[4, h1, :] = jnp.sum(vfr * dvi, axis=0, keepdims=True) + prod * (1.0 / CH)
            dxp[hs, lanes] += mf * dvf + mb * dvb
            vfe[hs, :] = (vf * wf[h1, :]).astype(BF)
            vbe[hs, :] = (vb * wb[h1, :]).astype(BF)
        dgb = jnp.where(low | up, dg_sum, 0.0).astype(BF)
        dbc[64:128, lanes] = nt(bt, dgb) + tn(sf[q], dye[0:inner, :]) + tn(sbb, dye[inner : 2 * inner, :])
        dbc[0:64, lanes] = nn(ct, dgb) + tn(dsb, vfe[...])
        grow = nt(dye[...], ct)
        srow = nt(vbe[...], bt)
        zb[q] = grow[inner : 2 * inner, :].astype(zb.dtype)
        for h in range(heads):
            hs = slice(64 * h, 64 * h + 64)
            dsf[hs, :] = dsf[hs, :] * etf[h : h + 1, :] + grow[hs, :]
            sb[hs, :] = sb[hs, :] * etb[h : h + 1, :] + srow[hs, :]
        ddt[0:16, lanes] = rows[0] * mask
        ddt[16:32, lanes] = rows[1] * mask
        dap[0:16, lanes] = running(rows[2], tri(lambda r, c: r >= c)) + jnp.sum(rows[4], axis=1, keepdims=True)
        dap[16:32, lanes] = running(rows[3], tri(lambda r, c: r > c)) + jnp.sum(rows[5], axis=1, keepdims=True)
    o = tn(ynt[...], wo[...])
    split_rows(core, o, own, oth)
    gacc[...] += nn(ynt[...], cot)

    @pl.when(i == last)
    def _():
        gacc[...] = gacc[...].T
        send_rows(meta, gacc, gwo)


def carry(meta, u, zt, alog, dxp, ddt, dap, dbc, zb, sbin, du, dz, dbias, dal, dsb, dvs, vbe, row):
    j = pl.program_id(0)
    length = meta[1]
    inner = dxp.shape[0]
    heads = inner // 64

    @pl.when(j == 0)
    def _():
        dsb[...] = jnp.zeros_like(dsb)
        dbias[...] = jnp.zeros_like(dbias)
        dal[...] = jnp.zeros_like(dal)
        row[...] = jnp.zeros_like(row)

    for q in range(BLK // CH):
        lanes = slice(q * CH, (q + 1) * CH)
        pos = j * BLK + q * CH + lax.broadcasted_iota(jnp.int32, (1, CH), 1)
        mask = jnp.where(pos < length, 1.0, 0.0)
        z = zt[:, lanes]
        mdt, a, cs = decays(z, alog[...], mask)
        ecb = cs[16:32] - a[16:32]
        etb = jnp.exp(cs[16:32, CH - 1 : CH])
        wb = jnp.exp(ecb)
        mw = mdt[16:32] * wb
        bu = u[inner : inner + 64, lanes]
        cu = u[inner + 64 : inner + 128, lanes]
        sgb = sigmoid(bu)
        sgc = sigmoid(cu)
        bt = (bu * sgb).astype(BF)
        dsb16 = dsb[...].astype(BF)
        dvs[...] = nn(dsb16, bt)
        for h in range(heads):
            hs = slice(64 * h, 64 * h + 64)
            h1 = slice(h, h + 1)
            uh = u[hs, lanes]
            sg = sigmoid(uh)
            x = uh * sg
            raw = dvs[hs, :]
            row[0, h1, :] = jnp.sum(x * raw, axis=0, keepdims=True) * wb[h1, :]
            prod = jnp.sum(dsb[hs, :] * sbin[q, hs, :].astype(F32), axis=0, keepdims=True)
            row[1, h1, :] = jnp.broadcast_to(jnp.sum(prod, axis=1, keepdims=True) * etb[h1, :], (1, CH))
            dx = dxp[hs, lanes] + raw * mw[h1, :]
            du[hs, lanes] = (dx * (sg * (1.0 + uh * (1.0 - sg)))).astype(BF)
            vbe[hs, :] = (x * mw[h1, :]).astype(BF)
        db = dbc[0:64, lanes] + tn(dsb16, vbe[...])
        du[inner : inner + 64, lanes] = (db * (sgb * (1.0 + bu * (1.0 - sgb)))).astype(BF)
        du[inner + 64 : inner + 128, lanes] = (dbc[64:128, lanes] * (sgc * (1.0 + cu * (1.0 - sgc)))).astype(BF)
        for h in range(heads):
            hs = slice(64 * h, 64 * h + 64)
            dsb[hs, :] = dsb[hs, :] * etb[h : h + 1, :] + zb[q, hs, :].astype(F32)
        dab = dap[16:32, lanes] + running(mdt[16:32] * row[0], tri(lambda r, c: r > c)) + row[1]
        da = jnp.concatenate([dap[0:16, lanes], dab], 0)
        dd = jnp.concatenate([ddt[0:16, lanes], ddt[16:32, lanes] + row[0] * mask], 0)
        dal[...] += da * a
        dzz = (dd - jnp.exp(alog[...]) * da) * sigmoid(z)
        dbias[...] += dzz
        dz[:, lanes] = dzz.astype(dz.dtype)


def lane_sums(v):
    ones = jnp.ones((8, v.shape[1]), F32)
    return lax.dot_general(ones, v, (((1,), (1,)), ((), ())), precision=HIGH, preferred_element_type=F32)[0:1]


def weigh(meta, du, nxt, ain, dgate, dz, nrm, taps, wt, gain, dgain, dbias, dal, dsk, cat, small, *refs):
    *gw, acc, flat, dtaps = refs
    j = pl.program_id(0)
    last = pl.num_programs(0) - 1
    inner = dgate.shape[0]
    conv = inner + 128

    @pl.when(j == 0)
    def _():
        dtaps[...] = jnp.zeros_like(dtaps)
        acc[...] = jnp.zeros_like(acc)

    cat[0:inner, :] = dgate[...]
    for g in range(0, conv, 128):
        cur = du[g : g + 128, :]
        after = nxt[g : g + 128, :]
        full = jnp.concatenate([cur, jnp.where(j == last, jnp.zeros_like(after), after)], 1)
        cur = cur.astype(F32)
        a = ain[g : g + 128, :].astype(F32)
        t = taps[g : g + 128, :]
        total = t[:, 3:4] * cur
        p = a * cur
        dtaps[3, g : g + 128, :] += p[:, 0:128] + p[:, 128:256]
        for k in (1, 2, 3):
            moved = pltpu.roll(full, BLK + 128 - k, 1)[:, 0:BLK].astype(F32)
            total = total + t[:, 3 - k : 4 - k] * moved
            p = a * moved
            dtaps[3 - k, g : g + 128, :] += p[:, 0:128] + p[:, 128:256]
        cat[inner + g : inner + g + 128, :] = total.astype(BF)
    cat[inner + conv : inner + conv + ZR, :] = dz[...]
    acc[...] += nn(cat[...], nrm[...])

    @pl.when(j == last)
    def _():
        flat[...] = acc[...].T
        send_rows(meta, flat, gw)
        small[...] = jnp.zeros_like(small)
        for k in range(4):
            small[k : k + 1, :] = lane_sums(dtaps[k])
        small[4:5, 0:inner] = lane_sums(dgain[...])
        norm = jnp.zeros((1, nrm.shape[1]), F32)
        for g in range(0, acc.shape[0], 32):
            norm = norm + jnp.sum(acc[g : g + 32, :] * wt[g : g + 32, :].astype(F32), axis=0, keepdims=True)
        small[5:6, 0:inner] = norm / gain[...]
        for i, ref in enumerate((dbias, dal, dsk)):
            small[6:7, 128 * i : 128 * i + ref.shape[0]] = lane_sums(ref[...])


def leave(meta, cat, wt, own, oth):
    gn = tn(cat[...], wt[...])
    split_rows(meta[0], gn, own, oth)


def _params():
    return pltpu.CompilerParams(dimension_semantics=("arbitrary",), vmem_limit_bytes=VMEM_LIMIT)


def full(shape):
    return pl.BlockSpec(shape, lambda j, *_: (0,) * len(shape))


def sds(shape, dt):
    return jax.ShapeDtypeStruct(shape, dt)


def run_enter(meta, xa, xb, pieces, near, gain, taps, bias, alog):
    nblk, width, dm = xa.shape
    length = 2 * nblk * width
    inner = taps.shape[0] - 128
    nk = BLK // (2 * width)
    nb = length // BLK
    rowsb = pl.BlockSpec((nk, width, dm), lambda j, *_: (j, 0, 0))
    colb = lambda n: pl.BlockSpec((n, BLK), lambda j, *_: (0, j))
    wrows = 2 * inner + 128 + ZR
    return pl.pallas_call(
        functools.partial(enter, near),
        grid_spec=pltpu.PrefetchScalarGridSpec(
            num_scalar_prefetch=1,
            grid=(nb,),
            in_specs=[rowsb, rowsb]
            + [full(p.shape) for p in pieces]
            + [full(gain.shape), full(taps.shape), full(bias.shape), full(alog.shape)],
            out_specs=[
                pl.BlockSpec((BLK, dm), lambda j, *_: (j, 0)),
                colb(inner),
                colb(inner + 128),
                colb(inner + 128),
                colb(ZR),
                pl.BlockSpec((BLK // CH, inner, 64), lambda j, *_: (j, 0, 0)),
                full((wrows, dm)),
                full((inner, dm)),
            ],
            scratch_shapes=[
                pltpu.VMEM((inner + 128, 128), F32),
                pltpu.VMEM((inner, 64), F32),
                pltpu.VMEM((inner, CH), BF),
                pltpu.VMEM((dm, pieces[0].shape[-1]), BF),
            ],
        ),
        out_shape=[
            sds((length, dm), BF),
            sds((inner, length), F32),
            sds((inner + 128, length), BF),
            sds((inner + 128, length), F32),
            sds((ZR, length), F32),
            sds((length // CH, inner, 64), BF),
            sds((wrows, dm), BF),
            sds((inner, dm), BF),
        ],
        compiler_params=_params(),
        cost_estimate=pl.CostEstimate(flops=2 * length * dm * wrows, bytes_accessed=30_000_000, transcendentals=4 * inner * length),
    )(meta, xa, xb, *pieces, gain, taps, bias, alog)


def run_mix(plan, meta, dskip, dya, dyb, wo, gate, u, zt, sf, gain, alog):
    nblk, width, dm = dya.shape
    length = 2 * nblk * width
    inner = gate.shape[0]
    nk = BLK // (2 * width)
    nb = length // BLK
    sent = message_shapes(plan, dm, inner)
    rowsb = pl.BlockSpec((nk, width, dm), lambda i, *_: (nb - 1 - i, 0, 0))
    colb = lambda n: pl.BlockSpec((n, BLK), lambda i, *_: (0, nb - 1 - i))
    stb = pl.BlockSpec((BLK // CH, inner, 64), lambda i, *_: (nb - 1 - i, 0, 0))
    return pl.pallas_call(
        mix,
        grid_spec=pltpu.PrefetchScalarGridSpec(
            num_scalar_prefetch=2,
            grid=(nb,),
            in_specs=[rowsb, rowsb, full((inner, dm)), colb(inner), colb(inner + 128), colb(ZR), stb, full(gain.shape), full(alog.shape)],
            out_specs=[
                rowsb,
                rowsb,
                colb(inner),
                colb(inner),
                colb(ZR),
                colb(ZR),
                colb(128),
                stb,
                stb,
                full((inner, CH)),
                full((16, CH)),
            ]
            + [full(m.shape) for m in sent],
            scratch_shapes=[
                pltpu.VMEM((inner, dm), F32),
                pltpu.VMEM((inner, BLK), F32),
                pltpu.VMEM((inner, BLK), BF),
                pltpu.VMEM((2 * inner, CH), F32),
                pltpu.VMEM((inner, CH), F32),
                pltpu.VMEM((2 * inner, CH), BF),
                pltpu.VMEM((inner, CH), BF),
                pltpu.VMEM((inner, CH), BF),
                pltpu.VMEM((inner, 64), F32),
                pltpu.VMEM((inner, 64), F32),
                pltpu.VMEM((6, 16, CH), F32),
                pltpu.VMEM((inner, CH), F32),
                pltpu.VMEM((inner, CH), F32),
                pltpu.VMEM((inner, CH), F32),
                pltpu.VMEM((inner, CH), BF),
                pltpu.VMEM((inner // 64, CH, CH), BF),
                pltpu.VMEM((inner // 64, CH, CH), BF),
                pltpu.VMEM((inner // 64, CH, CH), F32),
            ],
        ),
        out_shape=[
            sds((nblk, width, dm), F32),
            sds((nblk, width, dm), BF),
            sds((inner, length), BF),
            sds((inner, length), F32),
            sds((ZR, length), F32),
            sds((ZR, length), F32),
            sds((128, length), F32),
            sds((length // CH, inner, 64), BF),
            sds((length // CH, inner, 64), BF),
            sds((inner, CH), F32),
            sds((16, CH), F32),
        ]
        + sent,
        compiler_params=_params(),
        cost_estimate=pl.CostEstimate(flops=40 * 10**9, bytes_accessed=50_000_000, transcendentals=10**7),
    )(meta, dskip, dya, dyb, wo, gate, u, zt, sf, gain, alog)


def run_carry(meta, u, zt, alog, dxp, ddt, dap, dbc, zb, sbin):
    inner, length = dxp.shape
    nb = length // BLK
    colb = lambda n: pl.BlockSpec((n, BLK), lambda j, *_: (0, j))
    stb = pl.BlockSpec((BLK // CH, inner, 64), lambda j, *_: (j, 0, 0))
    return pl.pallas_call(
        carry,
        grid_spec=pltpu.PrefetchScalarGridSpec(
            num_scalar_prefetch=1,
            grid=(nb,),
            in_specs=[colb(inner + 128), colb(ZR), full(alog.shape), colb(inner), colb(ZR), colb(ZR), colb(128), stb, stb],
            out_specs=[colb(inner + 128), colb(ZR), full((ZR, CH)), full((ZR, CH))],
            scratch_shapes=[
                pltpu.VMEM((inner, 64), F32),
                pltpu.VMEM((inner, CH), F32),
                pltpu.VMEM((inner, CH), BF),
                pltpu.VMEM((2, 16, CH), F32),
            ],
        ),
        out_shape=[sds((inner + 128, length), BF), sds((ZR, length), BF), sds((ZR, CH), F32), sds((ZR, CH), F32)],
        compiler_params=_params(),
        cost_estimate=pl.CostEstimate(flops=10**9, bytes_accessed=30_000_000, transcendentals=10**6),
    )(meta, u, zt, alog, dxp, ddt, dap, dbc, zb, sbin)


def run_weigh(plan, meta, du, ain, dgate, dz, nrm, taps, *rest):
    inner, length = dgate.shape
    dm = nrm.shape[1]
    nb = length // BLK
    wrows = 2 * inner + 128 + ZR
    sent = message_shapes(plan, dm, wrows)
    colb = lambda n: pl.BlockSpec((n, BLK), lambda j, *_: (0, j))
    return pl.pallas_call(
        weigh,
        grid_spec=pltpu.PrefetchScalarGridSpec(
            num_scalar_prefetch=1,
            grid=(nb,),
            in_specs=[
                colb(inner + 128),
                pl.BlockSpec((inner + 128, 128), lambda j, *_: (0, jnp.minimum(2 * j + 2, 2 * nb - 1))),
                colb(inner + 128),
                colb(inner),
                colb(ZR),
                pl.BlockSpec((BLK, dm), lambda j, *_: (j, 0)),
                full(taps.shape),
            ]
            + [full(r.shape) for r in rest],
            out_specs=[colb(wrows), full((8, inner + 128))] + [full(m.shape) for m in sent],
            scratch_shapes=[
                pltpu.VMEM((wrows, dm), F32),
                pltpu.VMEM((dm, wrows), F32),
                pltpu.VMEM((4, inner + 128, 128), F32),
            ],
        ),
        out_shape=[sds((wrows, length), BF), sds((8, inner + 128), F32)] + sent,
        compiler_params=_params(),
        cost_estimate=pl.CostEstimate(flops=2 * length * dm * wrows, bytes_accessed=30_000_000, transcendentals=0),
    )(meta, du, du, ain, dgate, dz, nrm, taps, *rest)


def run_leave(meta, cat, wt, width):
    wrows, length = cat.shape
    dm = wt.shape[1]
    nk = BLK // (2 * width)
    nblk = length // (2 * width)
    rowsb = pl.BlockSpec((nk, width, dm), lambda j, *_: (j, 0, 0))
    return pl.pallas_call(
        leave,
        grid_spec=pltpu.PrefetchScalarGridSpec(
            num_scalar_prefetch=1,
            grid=(length // BLK,),
            in_specs=[
                pl.BlockSpec((wrows, BLK), lambda j, *_: (0, j)),
                full(wt.shape),
            ],
            out_specs=[rowsb, rowsb],
        ),
        out_shape=[sds((nblk, width, dm), F32), sds((nblk, width, dm), BF)],
        compiler_params=_params(),
        cost_estimate=pl.CostEstimate(flops=10**6, bytes_accessed=20_000_000, transcendentals=0),
    )(meta, cat, wt)


def permute_slots(rows, sender):
    def body(order, src, dst):
        for i in range(rows.shape[0]):
            dst[i] = src[order[i]]

    return pl.pallas_call(
        body,
        grid_spec=pltpu.PrefetchScalarGridSpec(
            num_scalar_prefetch=1, grid=(1,), in_specs=[full(rows.shape)], out_specs=full(rows.shape)
        ),
        out_shape=sds(rows.shape, rows.dtype),
        compiler_params=_params(),
    )(sender, rows)


WIDE = 60 * 10**9
SWAP = [(0, 1), (1, 0)]
CORNER = [(0, 0), (1, 2), (2, 1), (3, 3)]


def twin(v, axis):
    return lax.ppermute(v, axis, SWAP)


def corner(v):
    return lax.ppermute(v, ("core", "tensor"), CORNER)


def after(v, *others, wide=False):
    def body(*refs):
        pass

    space = pl.BlockSpec(memory_space=pl.ANY)
    return pl.pallas_call(
        body,
        in_specs=[space] * (1 + len(others)),
        out_specs=space,
        out_shape=sds(v.shape, v.dtype),
        input_output_aliases={0: 0},
        cost_estimate=pl.CostEstimate(flops=WIDE if wide else 0, bytes_accessed=0, transcendentals=0),
    )(v, *others)


def ahead_of(n, k):
    return [(i, (i + k) % n) for i in range(n)]


def gather_weights(pack, plan, moved):
    if plan is None:
        return [lax.all_gather(pack, ("z", "x", "tensor"), tiled=True)], [(0, 0, 0, 0)], moved, []
    ahead, behind, _ = plan
    got = [pack] + [lax.ppermute(pack, "z", ahead_of(ahead + behind, k)) for k in range(1, ahead + behind)]
    moved = after(moved, *got[1:])
    a, b = jnp.stack(got[:ahead]), jnp.stack(got[ahead:])
    a = after(a, moved, b, wide=True)
    b = after(b, a)
    by, bx = twin(b, "tensor"), twin(b, "x")
    ax, ay = twin(a, "x"), twin(a, "tensor")
    axy, bxy = twin(ax, "tensor"), twin(by, "x")
    near = [(0, ahead, 0, 0), (0, ahead, 1, 0), (0, ahead, 0, 1), (0, ahead, 1, 1)]
    far = [(ahead, behind, 0, 0), (ahead, behind, 0, 1), (ahead, behind, 1, 0), (ahead, behind, 1, 1)]
    return [a, ax, ay, axy, b, by, bx, bxy], near + far, moved, [ax, ay, axy, by, bx, bxy]


def add(kept, got):
    return kept.astype(F32) + got.astype(F32)


class ChipSum:
    def __init__(self, sent, plan):
        self.now, self.plan, self.got = sent, plan, []

    def send(self, step):
        s = self.now
        if self.plan is None:
            if step == 2:
                self.got = [lax.psum_scatter(s[0], ("z", "x", "tensor"), scatter_dimension=0, tiled=True)]
        elif step == 0:
            self.got = [twin(s[0], "x"), twin(s[2], "tensor")]
        elif step == 1:
            self.got = [twin(s[1], "tensor"), twin(s[3], "x")]
        else:
            n = len(s)
            self.got = [lax.ppermute(s[k], "z", ahead_of(n, k)) for k in range(1, n)]

    def hold(self, v):
        if self.plan is not None:
            at = 1 if len(self.now) == 4 and self.now[1].ndim == 4 else 0
            for i in (at, at + 2):
                self.now[i] = after(self.now[i], v)

    def add(self, step):
        s, g = self.now, self.got
        self.got = []
        if self.plan is None:
            self.now = g if step == 2 else s
        elif step == 0:
            a, b = add(s[1], g[0]), add(s[3], g[1])
            self.now = [a[0], a[1].astype(BF), b[0], b[1].astype(BF)]
        elif step == 1:
            a, b = add(s[0], g[0]), add(s[2], g[1])
            low = [a[k].astype(BF) for k in range(1, a.shape[0])] + [b[k].astype(BF) for k in range(b.shape[0])]
            self.now = [a[0]] + low
        else:
            total = s[0]
            for piece in g:
                total = add(total, piece)
            self.now = [total]


def unpack(grads, inner, heads):
    rows = grads.shape[0]

    def body(src, out, gate, mid, bc, dt):
        out[...] = src[:, 0:inner].astype(F32)
        gate[...] = src[:, inner : 2 * inner].astype(F32)
        mid[...] = src[:, 2 * inner : 3 * inner].astype(F32)
        bc[...] = src[:, 3 * inner : 3 * inner + 128].astype(F32)
        r = lax.broadcasted_iota(jnp.int32, (ZR, 2 * heads), 0)
        c = lax.broadcasted_iota(jnp.int32, (ZR, 2 * heads), 1)
        pick = jnp.where(r == (c & 1) * 16 + (c >> 1), 1.0, 0.0).astype(BF)
        dt[...] = nn(src[:, 3 * inner + 128 : 3 * inner + 128 + ZR], pick)

    shapes = [(rows, inner), (rows, inner), (rows, inner), (rows, 128), (rows, 2 * heads)]
    return pl.pallas_call(body, out_shape=[sds(s, F32) for s in shapes], compiler_params=pltpu.CompilerParams(vmem_limit_bytes=VMEM_LIMIT))(grads)


def pad_rows(fwd, bwd):
    h = fwd.shape[0]
    gap = jnp.zeros((16 - h,) + fwd.shape[1:], fwd.dtype)
    return jnp.concatenate([fwd, gap, bwd, gap], 0)


def shards(
    layer_in,
    out_grad,
    seq_lengths,
    slot_perm,
    norm_gain,
    w_gate,
    w_inner,
    w_bc,
    w_dt,
    conv_x,
    conv_bc,
    dt_bias,
    a_log,
    dskip,
    inner_gain,
    w_out,
):
    z, x, core, y = (lax.axis_index(a) for a in ("z", "x", "core", "tensor"))
    nz = lax.axis_size("z")
    group = ("tensor", "z", "x")
    seqs, _, width, dm = layer_in.shape
    inner = w_gate.shape[1]
    heads = a_log.shape[0]
    rows = w_gate.shape[0]
    slot = lax.axis_index(group)
    ids = jnp.arange(seqs, dtype=jnp.int32)
    sender = jnp.sum(jnp.where(slot_perm[None, :] == ids[:, None], ids[None, :], 0), axis=1)
    my_length = jnp.sum(jnp.where(slot_perm == slot, seq_lengths, 0))
    meta = jnp.stack([core, my_length, z, x, y, jnp.int32(nz)]).astype(jnp.int32)

    dt_cols = jnp.transpose(w_dt.reshape(rows, heads, 2), (0, 2, 1))
    dt_cols = jnp.pad(dt_cols, ((0, 0), (0, 0), (0, 16 - heads))).reshape(rows, ZR)
    pack = jnp.concatenate([w_out.T, w_gate, w_inner, w_bc, jnp.pad(dt_cols, ((0, 0), (0, 128 - ZR)))], 1)
    tiny = jnp.concatenate([dt_bias, a_log, dskip, jnp.zeros((inner - 4 * heads,), F32)])
    mine = corner(jnp.concatenate([conv_x, inner_gain[None], tiny[None], jnp.zeros((2, inner), F32)], 0))
    taps = jnp.concatenate([mine[0:4].T, conv_bc.T], 0)
    gain_u = mine[4][:, None]
    bias = mine[5, 0 : 2 * heads].reshape(heads, 2)
    alog = mine[5, 2 * heads : 3 * heads]
    skip = mine[5, 3 * heads : 4 * heads]
    bias = pad_rows(bias[:, 0:1], bias[:, 1:2])
    alog = pad_rows(alog[:, None], alog[:, None])

    ahead = nz // 2
    plan = (ahead, nz - ahead, rows) if rows % 16 == 0 else None
    moved = permute_slots(layer_in[:, 0], sender)
    pieces, near, moved, early = gather_weights(corner(pack), plan, moved)
    rows_own = lax.all_to_all(moved, group, 0, 0, tiled=True)
    dy = after(out_grad[:, 0], *early)
    rows_own = after(rows_own, *early)
    rows_oth = twin(rows_own, "core")
    cot_own = lax.all_to_all(dy, group, 0, 0, tiled=True)

    nrm, gate, ain, u, zt, sf, wt, wo = run_enter(meta, rows_own, rows_oth, pieces, near, norm_gain[None], taps, bias, alog)
    cot_own = after(cot_own, zt)
    cot_oth = twin(cot_own, "core")
    own, oth, dgate, dxp, ddt, dap, dbc, zb, sbin, dgain, dsk, *gwo = run_mix(
        plan, meta, skip, cot_own, cot_oth, wo, gate, u, zt, sf, gain_u, alog
    )
    position = (2 * jnp.arange(rows_own.shape[0], dtype=jnp.int32)[:, None] + core) * width
    position = position + jnp.arange(width, dtype=jnp.int32)[None, :]
    mask = (position < my_length).astype(F32)[..., None]
    xf = rows_own.astype(F32)
    oth = twin(oth, "core")
    out_grads = ChipSum(gwo, plan)
    out_grads.send(0)
    du, dz, dbias, dal = run_carry(meta, u, zt, alog, after(dxp, own, wide=True), ddt, dap, dbc, zb, sbin)
    out_rows = (xf + mask * add(after(own, du), oth)).astype(BF)
    output = lax.all_to_all(out_rows, group, 0, 0, tiled=True)
    out_grads.hold(out_rows)
    out_grads.add(0)
    out_grads.send(1)
    du = after(du, out_rows, wide=True)
    cat, small, *gw = run_weigh(
        plan, meta, du, ain, dgate, dz, nrm, taps, wt, norm_gain[None], dgain, dbias, dal, dsk
    )
    grads_in = ChipSum(gw, plan)
    grads_in.send(0)
    got = twin(small, "x")
    gown, goth = run_leave(meta, after(cat, small, wide=True), wt, width)

    gn = add(gown, twin(goth, "core"))
    inv = lax.rsqrt(jnp.mean(xf * xf, axis=-1, keepdims=True) + 1e-05)
    unit = xf * inv
    scaled = gn * norm_gain
    back = cot_own.astype(F32) + inv * (scaled - unit * jnp.mean(scaled * unit, axis=-1, keepdims=True))
    back = back.astype(BF)
    input_grad = lax.all_to_all(after(back, output), group, 0, 0, tiled=True)
    small = after(small, back) + got
    small = small + twin(small, "tensor")
    grads_in.hold(back)
    grads_in.add(0)
    grads_in.send(1)
    out_grads.hold(back)
    out_grads.add(1)
    out_grads.send(2)
    out_grads.add(2)
    k = 1
    while k < nz:
        small = small + lax.ppermute(small, "z", [(i, i ^ k) for i in range(nz)])
        k *= 2
    pair = twin(small, "core")
    grads_in.add(1)
    if plan is not None:
        grads_in.now = [after(v, input_grad) for v in grads_in.now]
    grads_in.send(2)
    grads_in.add(2)
    gw_sum, gwo_sum = grads_in.now[0], out_grads.now[0]

    bc_part = gw_sum[:, 2 * inner : 2 * inner + 128]
    bc_part = bc_part + twin(bc_part, "core")
    grads = jnp.concatenate([gwo_sum, gw_sum[:, : 2 * inner], bc_part, gw_sum[:, 2 * inner + 128 :]], 1)
    grads = corner(grads.astype(BF))
    out_sum, gate_sum, inner_sum, bc_sum, dt_sum = unpack(grads, inner, heads)

    here = jnp.where(core == y, small, pair)
    joint = small + pair
    heads_of = lambda at: here[6, at : at + ZR].reshape(2, 16)[:, :heads]
    return (
        output[:, None],
        input_grad[:, None],
        joint[5, :inner],
        gate_sum,
        inner_sum,
        bc_sum,
        dt_sum,
        here[0:4, :inner],
        joint[0:4, inner:],
        heads_of(0).T.reshape(2 * heads),
        heads_of(128).sum(0),
        here[6, 256 : 256 + heads],
        here[4, :inner],
        out_sum.T,
    )


def solution(mesh):
    dp, tensor = mesh.devices.shape
    fine = Mesh(mesh.devices.reshape(dp // 4, 2, 2, tensor), ("z", "x", "core", "tensor"))
    d = ("z", "x", "core")
    t = "tensor"
    return jax.shard_map(
        shards,
        mesh=fine,
        in_specs=(
            P(None, t, d, None),
            P(None, t, d, None),
            P(),
            P(),
            P(),
            P(d, t),
            P(d, t),
            P(d, None),
            P(d, t),
            P(None, t),
            P(),
            P(t),
            P(t),
            P(t),
            P(t),
            P(t, d),
        ),
        out_specs=(
            P(None, t, d, None),
            P(None, t, d, None),
            P(),
            P(d, t),
            P(d, t),
            P(d, None),
            P(d, t),
            P(None, t),
            P(),
            P(t),
            P(t),
            P(t),
            P(t),
            P(t, d),
        ),
        check_vma=False,
    )
```
